256 devices in a mesh: batch: 16 (over z, y_hi), group: 16 (over y_lo, x, core).
Axes of the slice: x: 4, y: 4 (y_hi: 2, y_lo: 2; y = y_hi * 2 + y_lo), z: 8, core: 2. Of those that a mesh axis runs over, the one named last changes fastest.
Arguments:
- picture_embeds: bfloat16 [16384, 1152], P(('batch', 'group'))
- caption_embeds: bfloat16 [16384, 1152], P(('batch', 'group'))
- positive_caption_ids: int32 [16384], P(('batch', 'group')), may hold values from 0 to 16383, as said below
- logit_multiplier: float32 [1], replicated, may hold values from 11 to 16
- logit_shift: float32 [1], replicated, may hold values from -0.5 to 0.5
Outputs:
- image_grad_t: bfloat16 [1152, 16384], P('group', 'batch')
- text_grad: float32 [16384, 1152], P(('batch', 'group'))
The draws below stay inside these ranges and needn't reach their ends.
Inputs may be any that keep to these rules, and one draw needn't show every extreme that they name: `positive_caption_ids`: labels is a permutation: each text is the positive of exactly one image.
All inputs are finite; a program needn't handle non-finite values.
Results may differ from the reference program's by a relative error of at most 0.008.
Values may be sent and summed in bfloat16 or wider, within the bound.
A program may use at most 64 MiB of HBM per device.

```python
import math
import jax
import jax.numpy as jnp
from jax import lax

D = 1152
ROWS = 1024
NT = 16384
NI = 16384


def shared_pairs(key):
    positive_caption_ids = jax.random.permutation(jax.random.fold_in(key, 101), NI).astype(jnp.int32)
    shuffled = jax.random.permutation(jax.random.fold_in(key, 104), NT).astype(jnp.int32)
    cluster_of = shuffled // 16
    centers = jax.random.normal(jax.random.fold_in(key, 105), (NT // 16, D), jnp.float32)
    strength = jax.random.uniform(jax.random.fold_in(key, 106), (NT // 16, 1), jnp.float32, 0.35, 0.65)
    individual = jax.random.normal(jax.random.fold_in(key, 102), (NT, D), jnp.float32)
    mixing = strength[cluster_of]
    anchor = jnp.sqrt(mixing) * centers[cluster_of] + jnp.sqrt(1.0 - mixing) * individual
    caption_count = jnp.exp(jax.random.uniform(jax.random.fold_in(key, 103), (1, D), jnp.float32, 0.0, math.log(4.0)))
    return (positive_caption_ids, anchor * caption_count)


def draw_caption_embeds(key, part):
    positive_caption_ids, anchor = shared_pairs(key)
    return (0.03 * anchor).astype(jnp.bfloat16)


def draw_positive_caption_ids(key, part):
    positive_caption_ids, anchor = shared_pairs(key)
    return positive_caption_ids


def draw_picture_embeds(key, part):
    positive_caption_ids, anchor = shared_pairs(key)
    key = jax.random.fold_in(key, 3)
    caption_count = jnp.exp(jax.random.uniform(jax.random.fold_in(key, 2), (1, D), jnp.float32, 0.0, math.log(4.0)))
    jitter = jax.random.normal(jax.random.fold_in(key, 1), (NI, D), jnp.float32)
    return (0.03 * (anchor[positive_caption_ids] + jitter) * caption_count).astype(jnp.bfloat16)


def setup_inputs(seed: int = 0) -> dict:
    seeds = jax.random.split(jax.random.key(seed), 6)
    return {
        "picture_embeds": draw_picture_embeds(jax.random.fold_in(seeds[5], 71), 0),
        "caption_embeds": draw_caption_embeds(jax.random.fold_in(seeds[5], 71), 0),
        "positive_caption_ids": draw_positive_caption_ids(jax.random.fold_in(seeds[5], 71), 0),
        "logit_multiplier": jnp.clip(jnp.exp(jax.random.uniform(seeds[3], (1,), jnp.float32, math.log(11.0), math.log(16.0))), 11.0, 16.0),
        "logit_shift": jnp.clip(jax.random.uniform(seeds[4], (1,), jnp.float32, -0.5, 0.5), -0.5, 0.5),
    }


epsilon = 1e-06

def unit_rows(values):
    wide = values.astype(jnp.float32)
    inverse = lax.rsqrt(lax.optimization_barrier(jnp.sum(wide * wide, axis=1, keepdims=True)) + epsilon)
    return (wide * inverse, inverse)

def tile_factor(picture_unit_vectors, caption_unit_vectors, match_grid, logit_multiplier, logit_shift):
    cross_cosine_grid = jnp.dot(picture_unit_vectors, caption_unit_vectors.T, preferred_element_type=jnp.float32)
    cross_raw_similarity = logit_multiplier * cross_cosine_grid + logit_shift
    caption_count = jnp.arange(caption_unit_vectors.shape[0], dtype=jnp.int32)
    match_polarity = jnp.where(match_grid[:, None] == caption_count[None, :], 1.0, -1.0).astype(jnp.float32)
    return (logit_multiplier * -match_polarity * jax.nn.sigmoid(-match_polarity * cross_raw_similarity)).astype(jnp.bfloat16)

def reference(picture_embeds, caption_embeds, positive_caption_ids, logit_multiplier, logit_shift):
    multiplier_scalar = logit_multiplier[0]
    shift_scalar = logit_shift[0]
    text_unit32, text_inverse = unit_rows(caption_embeds)
    caption_unit_vectors = text_unit32.astype(jnp.bfloat16)
    blocks = picture_embeds.reshape(NI // ROWS, ROWS, D)
    label_blocks = positive_caption_ids.reshape(NI // ROWS, ROWS)

    def advance(state, inputs):
        block, match_grid = inputs
        unit32, inverse = unit_rows(block)
        picture_unit_vectors = unit32.astype(jnp.bfloat16)
        entry_factor = tile_factor(picture_unit_vectors, caption_unit_vectors, match_grid, multiplier_scalar, shift_scalar)
        image_up = jnp.dot(entry_factor, caption_unit_vectors, preferred_element_type=jnp.float32)
        image_back = (image_up - unit32 * lax.optimization_barrier(jnp.sum(unit32 * image_up, axis=1, keepdims=True))) * inverse
        state = state + jnp.dot(entry_factor.T, picture_unit_vectors, preferred_element_type=jnp.float32)
        return (state, image_back.astype(jnp.bfloat16))
    text_up, backs = lax.scan(advance, jnp.zeros((NT, D), jnp.float32), (blocks, label_blocks))
    image_grad_t = backs.reshape(NI, D).T
    text_grad = (text_up - text_unit32 * lax.optimization_barrier(jnp.sum(text_unit32 * text_up, axis=1, keepdims=True))) * text_inverse
    return (image_grad_t, text_grad)
```

```python
import functools

import jax
import jax.numpy as jnp
from jax import lax
from jax.experimental import pallas as pl
from jax.experimental.pallas import tpu as pltpu
from jax.sharding import PartitionSpec as P

EPS = 1e-06
ROWS = 64
HALF = ROWS // 2
D = 1152
SIDE = 4
NZ = 8
FEAT = D // 8
PART = D // 16
LOG2E = 1.4426950408889634
f32 = jnp.float32
bf16 = jnp.bfloat16


def rdma(src, dst, ssem, rsem, dev):
    return pltpu.make_async_remote_copy(
        src_ref=src, dst_ref=dst, send_sem=ssem, recv_sem=rsem,
        device_id=dev, device_id_type=pl.DeviceIdType.MESH)


def unit_rows(values):
    wide = values.astype(f32)
    inverse = lax.rsqrt(jnp.sum(wide * wide, axis=1, keepdims=True) + EPS)
    return wide * inverse, inverse


def kernel(pic, cap, lab, mul, shift, img_out, txt_out,
           U, M, T, Ut, Tt, W, tacc, svec, own, sib_out, sib_in,
           tstage, trecv, G, rbh, rbf, rah, raf, r1, fin, fin_in,
           us, ur, ms, mr, zs, zr, bs, br, ts, tr, gs, gr, xs, xr):
    batch = lax.axis_index("batch")
    group = lax.axis_index("group")
    z, yh = batch // 2, batch % 2
    core = group % 2
    x = (group // 2) % SIDE
    y = yh * 2 + group // (2 * SIDE)
    m = mul[0]
    b = shift[0]

    def dev(x_, y_, z_, c_):
        return (z_ * 2 + y_ // 2, ((y_ % 2) * SIDE + x_) * 2 + c_)

    first = core == 0
    pa = jnp.where(first, x, y)
    pb = jnp.where(first, y, x)

    def slot(ka, kb):
        a_ = (pa + ka) % SIDE
        b_ = (pb + kb) % SIDE
        return jnp.where(first, b_ * SIDE + a_, a_ * SIDE + b_)

    def plane(ka, kb):
        a_ = (pa + ka) % SIDE
        b_ = (pb + kb) % SIDE
        return dev(jnp.where(first, a_, b_), jnp.where(first, b_, a_), z, core)

    a_dev = (plane(1, 0), plane(SIDE - 1, 0))
    b_dev = (plane(0, 1), plane(0, SIDE - 1))
    z_dev = (dev(x, y, (z + 1) % NZ, core), dev(x, y, (z + NZ - 1) % NZ, core))
    sib = dev(x, y, z, 1 - core)

    barrier = pltpu.get_barrier_semaphore()
    for d in (*a_dev, *b_dev, *z_dev, sib):
        pl.semaphore_signal(barrier, inc=1, device_id=d, device_id_type=pl.DeviceIdType.MESH)

    me = slot(0, 0)
    p_unit, p_inv = unit_rows(pic[...])
    U[me] = p_unit.astype(bf16).reshape(2, HALF, D)
    t_unit, t_inv = unit_rows(cap[...])
    T[0] = t_unit.astype(bf16).reshape(2, HALF, D)
    spread = jnp.broadcast_to(p_inv, (ROWS, 128))
    inv_lane = jnp.concatenate([spread, spread], axis=0).T[0:8]
    lab_row = lab[...].astype(f32)
    lab_lane = jnp.broadcast_to(jnp.concatenate([lab_row, lab_row], axis=1), (8, 128))
    row8 = lax.broadcasted_iota(jnp.int32, (8, 128), 0)
    lane8 = lax.broadcasted_iota(jnp.int32, (8, 128), 1)
    meta = jnp.where(row8 == 0, inv_lane, jnp.where(row8 == 1, lab_lane, 0.0))
    M[me] = jnp.where(lane8 // ROWS == x % 2, meta, 0.0)

    pl.semaphore_wait(barrier, 7)

    started = []

    def go(copy):
        copy.start()
        started.append(copy)

    def img_full(i, j, slot_, dst):
        go(rdma(U.at[slot_], U.at[slot_], us.at[i], ur.at[i], dst))
        go(rdma(M.at[slot_], M.at[slot_], ms.at[j], mr.at[j], dst))

    def img_half(i, slot_, hf, dst):
        go(rdma(U.at[slot_, hf], U.at[slot_, hf], us.at[i], ur.at[i], dst))

    def meta_only(j, slot_, dst):
        go(rdma(M.at[slot_], M.at[slot_], ms.at[j], mr.at[j], dst))

    def got_img(i, slot_):
        rdma(U.at[slot_], U.at[slot_], us.at[i], ur.at[i], sib).wait_recv()

    def got_half(i, slot_, hf):
        rdma(U.at[slot_, hf], U.at[slot_, hf], us.at[i], ur.at[i], sib).wait_recv()

    def got_meta(j, slot_):
        rdma(M.at[slot_], M.at[slot_], ms.at[j], mr.at[j], sib).wait_recv()

    def b1(ka):
        img_full(4 + 2 * ka, 3 + 2 * ka, slot(ka, 0), b_dev[0])
        img_full(5 + 2 * ka, 4 + 2 * ka, slot(ka, 0), b_dev[1])

    def b2(ka):
        before, after = slot(ka, SIDE - 1), slot(ka, 1)
        got_img(4 + 2 * ka, before)
        img_half(12 + 2 * ka, before, 0, b_dev[0])
        got_meta(3 + 2 * ka, before)
        meta_only(11 + ka, before, b_dev[0])
        got_img(5 + 2 * ka, after)
        img_half(13 + 2 * ka, after, 1, b_dev[1])
        got_meta(4 + 2 * ka, after)

    def b3(ka):
        far = slot(ka, 2)
        got_half(12 + 2 * ka, far, 0)
        got_half(13 + 2 * ka, far, 1)
        got_meta(11 + ka, far)

    def to_sib(k):
        go(rdma(T.at[k], T.at[NZ + k], bs.at[k], br.at[k], sib))

    def z_send(i, k, d):
        to = (k + NZ - 1) % NZ if d == 0 else (k + 1) % NZ
        go(rdma(T.at[k], T.at[to], zs.at[i], zr.at[i], z_dev[d]))

    def z_got(i, k):
        rdma(T.at[k], T.at[k], zs.at[i], zr.at[i], sib).wait_recv()

    z_send(0, 0, 0)
    z_send(1, 0, 1)
    img_full(0, 0, me, a_dev[0])
    img_full(1, 1, me, a_dev[1])
    b1(0)
    to_sib(0)
    before, after = slot(SIDE - 1, 0), slot(1, 0)
    got_img(0, before)
    img_half(2, before, 0, a_dev[0])
    got_meta(0, before)
    meta_only(2, before, a_dev[0])
    b1(3)
    got_img(1, after)
    img_half(3, after, 1, a_dev[1])
    got_meta(1, after)
    b1(1)
    z_got(0, 7)
    z_send(2, 7, 0)
    to_sib(7)
    z_got(1, 1)
    z_send(3, 1, 1)
    to_sib(1)
    b2(0)
    far = slot(2, 0)
    got_half(2, far, 0)
    got_half(3, far, 1)
    got_meta(2, far)
    b1(2)
    z_got(2, 6)
    z_send(4, 6, 0)
    to_sib(6)
    z_got(3, 2)
    z_send(5, 2, 1)
    to_sib(2)
    b2(3)
    b2(1)
    z_got(4, 5)
    go(rdma(T.at[5, 0], T.at[4, 0], zs.at[6], zr.at[6], z_dev[0]))
    to_sib(5)
    z_got(5, 3)
    go(rdma(T.at[3, 1], T.at[4, 1], zs.at[7], zr.at[7], z_dev[1]))
    to_sib(3)
    b2(2)
    for ka in (0, 3, 1, 2):
        b3(ka)
    rdma(T.at[4, 0], T.at[4, 0], zs.at[6], zr.at[6], sib).wait_recv()
    rdma(T.at[4, 1], T.at[4, 1], zs.at[7], zr.at[7], sib).wait_recv()
    to_sib(4)
    for k in (0, 7, 1, 6, 2, 5, 3, 4):
        rdma(T.at[NZ + k], T.at[NZ + k], bs.at[k], br.at[k], sib).wait_recv()

    @pl.loop(0, 4)
    def _(q):
        Ut[q] = U[pl.ds(q * 4, 4)].reshape(4 * ROWS, D).T

    for q in range(4):
        Tt[:, q * 256:(q + 1) * 256] = T[4 * q:4 * q + 4].reshape(4 * ROWS, D).T

    base = yh * 1024 + (group // 2) * 128
    k1 = m * LOG2E
    k2 = b * LOG2E

    def lane_vec(q, r):
        lo = M[q * 4, r:r + 1] + M[q * 4 + 1, r:r + 1]
        hi = M[q * 4 + 2, r:r + 1] + M[q * 4 + 3, r:r + 1]
        return jnp.concatenate([lo, hi], axis=1)

    tacc[...] = jnp.zeros_like(tacc)
    svec[...] = jnp.zeros_like(svec)

    @pl.loop(0, 8)
    def _(step):
        q = step // 2
        hf = step % 2
        rows = T[pl.ds(hf * NZ, NZ)].reshape(512, D)
        images = U[pl.ds(q * 4, 4)].reshape(256, D)
        cos = lax.dot_general(rows, images, (((1,), (1,)), ((), ())), preferred_element_type=f32)
        r = lax.broadcasted_iota(jnp.int32, (512, 1), 0)
        owner = jnp.where(hf == 0, core, 1 - core)
        ids = ((z + (r >> 6)) & 7) * 2048 + (base + owner * ROWS) + (r & 63)
        match = ids.astype(f32) == lane_vec(q, 1)
        logit = cos * k1 + k2
        e = jnp.exp2(jnp.where(match, logit, -logit))
        w = (jnp.where(match, -m, m) / (1.0 + e)).astype(bf16)
        at = pl.multiple_of(q * 256, 256)
        W[pl.ds(pl.multiple_of(hf * 512, 512), 512), pl.ds(at, 256)] = w
        wc = w.astype(f32) * cos
        svec[q] += jnp.broadcast_to(jnp.sum(wc, axis=0, keepdims=True), (8, 256))
        tacc[hf] += wc[:, :128] + wc[:, 128:]

    images = U[...].reshape(1024, D)

    def text_part(hf, lo, n):
        up = jnp.dot(W[hf * 512:hf * 512 + 512, :], images[:, lo:lo + n], preferred_element_type=f32)
        along = jnp.sum(tacc[hf], axis=1, keepdims=True)
        return up - T[hf * NZ:hf * NZ + NZ, :, :, lo:lo + n].reshape(512, n).astype(f32) * along

    cuts = [(0, 256), (256, 256), (512, 256), (768, 256), (1024, 128)]
    for lo, n in cuts:
        sib_out[:, :, :, lo:lo + n] = text_part(1, lo, n).astype(bf16).reshape(NZ, 2, HALF, n)
    swap = rdma(sib_out, sib_in, xs.at[0], xr.at[0], sib)
    go(swap)
    for lo, n in cuts:
        own[:, :, :, lo:lo + n] = text_part(0, lo, n).reshape(NZ, 2, HALF, n)

    @pl.loop(0, 4)
    def _(q):
        at = pl.multiple_of(q * 256, 256)
        up = jnp.dot(Tt[...], W[:, pl.ds(at, 256)], preferred_element_type=f32)
        along = svec[q][0:1]
        inv = lane_vec(q, 0)
        for g in range(8):
            lo = g * FEAT
            part = (up[lo:lo + FEAT] - Ut[q, lo:lo + FEAT].astype(f32) * along) * inv
            G[(q // 2) * 8 + g, q % 2] = part.astype(bf16)

    def text_sum(k):
        return own[k] + sib_in[k].astype(f32)

    def t_copy(d, i):
        src, dst = tstage.at[d, i], trecv.at[d, i]
        if i == 0:
            src, dst = tstage.at[d, 0, d], trecv.at[d, 0, d]
        return rdma(src, dst, ts.at[4 * d + i], tr.at[4 * d + i], z_dev[d])

    def t_step(i):
        for d in (0, 1):
            k = 4 - i if d == 0 else 4 + i
            if i == 0:
                tstage[d, 0, d] = (own[4, d] + sib_in[4, d].astype(f32)).astype(bf16)
            else:
                t_copy(d, i - 1).wait_recv()
                if i == 1:
                    tstage[d, 1, d] = (own[k, d] + sib_in[k, d].astype(f32)
                                       + trecv[d, 0, d].astype(f32)).astype(bf16)
                    tstage[d, 1, 1 - d] = (own[k, 1 - d] + sib_in[k, 1 - d].astype(f32)).astype(bf16)
                else:
                    tstage[d, i] = (text_sum(k) + trecv[d, i - 1].astype(f32)).astype(bf16)
            go(t_copy(d, i))

    def gb_first(ka):
        for d in (0, 1):
            go(rdma(G.at[slot(ka, 2), d], rbh.at[ka, d], gs.at[2 * ka + d], gr.at[2 * ka + d], b_dev[d]))

    def gb_second(ka):
        for d in (0, 1):
            at = slot(ka, 1 if d == 0 else SIDE - 1)
            rdma(rbh.at[ka, d], rbh.at[ka, d], gs.at[2 * ka + d], gr.at[2 * ka + d], sib).wait_recv()
            G[at, d] = (G[at, d].astype(f32) + rbh[ka, d].astype(f32)).astype(bf16)
            go(rdma(G.at[at], rbf.at[ka, d], gs.at[8 + 2 * ka + d], gr.at[8 + 2 * ka + d], b_dev[d]))

    def gb_last(ka):
        for d in (0, 1):
            i = 8 + 2 * ka + d
            rdma(rbf.at[ka, d], rbf.at[ka, d], gs.at[i], gr.at[i], sib).wait_recv()
        return G[slot(ka, 0)].astype(f32) + rbf[ka, 0].astype(f32) + rbf[ka, 1].astype(f32)

    order = (2, 1, 3, 0)
    for ka in order:
        gb_first(ka)
    swap.wait_recv()
    t_step(0)
    for ka in order:
        gb_second(ka)
    t_step(1)
    r1[0] = gb_last(2).astype(bf16)
    for d in (0, 1):
        go(rdma(r1.at[0, d], rah.at[d], gs.at[16 + d], gr.at[16 + d], a_dev[d]))
    t_step(2)
    for d, ka in ((0, 1), (1, 3)):
        part = gb_last(ka)
        rdma(rah.at[d], rah.at[d], gs.at[16 + d], gr.at[16 + d], sib).wait_recv()
        r1[1 + d, d] = (part[d] + rah[d].astype(f32)).astype(bf16)
        r1[1 + d, 1 - d] = part[1 - d].astype(bf16)
        go(rdma(r1.at[1 + d], raf.at[d], gs.at[18 + d], gr.at[18 + d], a_dev[d]))
    t_step(3)
    total = gb_last(0)
    for d in (0, 1):
        rdma(raf.at[d], raf.at[d], gs.at[18 + d], gr.at[18 + d], sib).wait_recv()
    total = total + raf[0].astype(f32) + raf[1].astype(f32)
    for c in (0, 1):
        fin[c] = total[:, c * PART:(c + 1) * PART]
    last = rdma(fin.at[1 - core], fin_in, xs.at[1], xr.at[1], sib)
    go(last)

    for d in (0, 1):
        t_copy(d, 3).wait_recv()
    txt = text_sum(0) + trecv[0, 3].astype(f32) + trecv[1, 3].astype(f32)
    txt_out[...] = txt.reshape(ROWS, D) * t_inv

    last.wait_recv()
    mine = fin[core]
    other = fin_in[...]
    even = jnp.where(first, mine, other)
    odd = jnp.where(first, other, mine)
    blocks = []
    for g in range(8):
        lo = (g % 4) * ROWS
        blocks += [even[g // 4][:, lo:lo + ROWS], odd[g // 4][:, lo:lo + ROWS]]
    img_out[...] = jnp.concatenate(blocks, axis=1).astype(bf16)

    for copy in started:
        copy.wait_send()


def local(picture_embeds, caption_embeds, positive_caption_ids, logit_multiplier, logit_shift):
    vmem = pl.BlockSpec(memory_space=pltpu.VMEM)
    smem = pl.BlockSpec(memory_space=pltpu.SMEM)
    dma = pltpu.SemaphoreType.DMA
    scratch = [
        pltpu.VMEM((16, 2, HALF, D), bf16),
        pltpu.VMEM((16, 8, 128), f32),
        pltpu.VMEM((16, 2, HALF, D), bf16),
        pltpu.VMEM((4, D, 256), bf16),
        pltpu.VMEM((D, 1024), bf16),
        pltpu.VMEM((1024, 1024), bf16),
        pltpu.VMEM((2, 512, 128), f32),
        pltpu.VMEM((4, 8, 256), f32),
        pltpu.VMEM((NZ, 2, HALF, D), f32),
        pltpu.VMEM((NZ, 2, HALF, D), bf16),
        pltpu.VMEM((NZ, 2, HALF, D), bf16),
        pltpu.VMEM((2, 4, 2, HALF, D), bf16),
        pltpu.VMEM((2, 4, 2, HALF, D), bf16),
        pltpu.VMEM((16, 2, FEAT, 256), bf16),
        pltpu.VMEM((4, 2, FEAT, 256), bf16),
        pltpu.VMEM((4, 2, 2, FEAT, 256), bf16),
        pltpu.VMEM((2, FEAT, 256), bf16),
        pltpu.VMEM((2, 2, FEAT, 256), bf16),
        pltpu.VMEM((3, 2, FEAT, 256), bf16),
        pltpu.VMEM((2, 2, PART, 256), f32),
        pltpu.VMEM((2, PART, 256), f32),
        dma((20,)), dma((20,)),
        dma((15,)), dma((15,)),
        dma((8,)), dma((8,)),
        dma((8,)), dma((8,)),
        dma((8,)), dma((8,)),
        dma((20,)), dma((20,)),
        dma((2,)), dma((2,)),
    ]
    return pl.pallas_call(
        kernel,
        out_shape=(jax.ShapeDtypeStruct((PART, 1024), bf16), jax.ShapeDtypeStruct((ROWS, D), f32)),
        in_specs=[vmem, vmem, vmem, smem, smem],
        out_specs=(vmem, vmem),
        scratch_shapes=scratch,
        compiler_params=pltpu.CompilerParams(
            collective_id=0, has_side_effects=True, vmem_limit_bytes=56 * 2**20),
        cost_estimate=pl.CostEstimate(flops=7 * 10**9, bytes_accessed=10**6, transcendentals=2**20),
    )(picture_embeds, caption_embeds, positive_caption_ids.reshape(1, ROWS), logit_multiplier, logit_shift)


def solution(mesh):
    placed = (P(("batch", "group"), None), P(("batch", "group"), None), P(("batch", "group")), P(), P())
    return jax.shard_map(
        local, mesh=mesh, in_specs=placed,
        out_specs=(P("group", "batch"), P(("batch", "group"), None)), check_vma=False)
```

```python
import functools

import jax
import jax.numpy as jnp
from jax import lax
from jax.experimental import pallas as pl
from jax.experimental.pallas import tpu as pltpu
from jax.sharding import PartitionSpec as P

EPS = 1e-06
ROWS = 64
HALF = ROWS // 2
D = 1152
SIDE = 4
NZ = 8
FEAT = D // 8
PART = D // 16
LOG2E = 1.4426950408889634
f32 = jnp.float32
bf16 = jnp.bfloat16


def rdma(src, dst, ssem, rsem, dev):
    return pltpu.make_async_remote_copy(
        src_ref=src, dst_ref=dst, send_sem=ssem, recv_sem=rsem,
        device_id=dev, device_id_type=pl.DeviceIdType.MESH)


def unit_rows(values):
    wide = values.astype(f32)
    inverse = lax.rsqrt(jnp.sum(wide * wide, axis=1, keepdims=True) + EPS)
    return wide * inverse, inverse
VMEM_MIB = 48

ORDER = (4, 3, 5, 2, 6, 1, 7, 0)
PLACE = {k: i for i, k in enumerate(ORDER)}
N_SEM = 160


def kernel(pic_hbm, cap_hbm, lab, mul, shift, img_out, txt_out,
           pic, cap, U, M, T, Ut, Tt, W, tacc, svec, own, sib_out, sib_in,
           tstage, trecv, G, rbh, rbf, ra, r1, fin, fin_in, ssem, rsem, lsem):
    batch = lax.axis_index("batch")
    group = lax.axis_index("group")
    z, yh = batch // 2, batch % 2
    core = group % 2
    x = (group // 2) % SIDE
    y = yh * 2 + group // (2 * SIDE)
    m = mul[0]
    shift0 = shift[0]
    first = core == 0
    pa = jnp.where(first, x, y)
    pb = jnp.where(first, y, x)

    def dev(x_, y_, z_, c_):
        return (z_ * 2 + y_ // 2, ((y_ % 2) * SIDE + x_) * 2 + c_)

    def slot(ka, kb):
        return (pb + kb) % SIDE * SIDE + (pa + ka) % SIDE

    def plane(ka, kb):
        a_ = (pa + ka) % SIDE
        b_ = (pb + kb) % SIDE
        return dev(jnp.where(first, a_, b_), jnp.where(first, b_, a_), z, core)

    z_dev = (dev(x, y, (z + 1) % NZ, core), dev(x, y, (z + NZ - 1) % NZ, core))
    b_dev = (plane(0, 1), plane(0, SIDE - 1))
    sib = dev(x, y, z, 1 - core)

    loads = (pltpu.make_async_copy(pic_hbm, pic, lsem.at[0]),
             pltpu.make_async_copy(cap_hbm, cap, lsem.at[1]))
    for load in loads:
        load.start()
    barrier = pltpu.get_barrier_semaphore()
    partners = (*z_dev, *b_dev, plane(1, 0), plane(3, 0), plane(2, 0), sib)
    for d in partners:
        pl.semaphore_signal(barrier, inc=1, device_id=d, device_id_type=pl.DeviceIdType.MESH)

    table = {}
    started = []

    def at(key):
        i = table.setdefault(key, len(table))
        assert i < N_SEM
        return i

    def send(key, src, dst, to):
        copy = rdma(src, dst, ssem.at[at(key)], rsem.at[at(key)], to)
        copy.start()
        started.append(copy)

    def got(key, dst):
        rdma(dst, dst, ssem.at[at(key)], rsem.at[at(key)], sib).wait_recv()

    me = slot(0, 0)
    loads[1].wait()
    t_unit, t_inv = unit_rows(cap[...])
    T[PLACE[0]] = t_unit.astype(bf16).reshape(2, HALF, D)
    loads[0].wait()
    p_unit, p_inv = unit_rows(pic[...])
    U[me] = p_unit.astype(bf16).reshape(2, HALF, D)
    spread = jnp.broadcast_to(p_inv, (ROWS, 128))
    inv_lane = jnp.concatenate([spread, spread], axis=0).T[0:8]
    lab_row = lab[...].astype(f32)
    lab_lane = jnp.broadcast_to(jnp.concatenate([lab_row, lab_row], axis=1), (8, 128))
    row8 = lax.broadcasted_iota(jnp.int32, (8, 128), 0)
    lane8 = lax.broadcasted_iota(jnp.int32, (8, 128), 1)
    meta = jnp.where(row8 == 0, inv_lane, jnp.where(row8 == 1, lab_lane, 0.0))
    M[me] = jnp.where(lane8 // ROWS == pa % 2, meta, 0.0)

    pl.semaphore_wait(barrier, len(partners))

    def send_u(ka, kb, hf, da, db):
        s = slot(ka, kb)
        send(("u", (ka - da) % SIDE, (kb - db) % SIDE, hf), U.at[s, hf], U.at[s, hf], plane(da, db))

    def got_u(ka, kb, hf):
        got(("u", ka, kb, hf), U.at[slot(ka, kb), hf])

    def send_m(ka, kb, da, db):
        s = slot(ka, kb)
        send(("m", (ka - da) % SIDE, (kb - db) % SIDE), M.at[s], M.at[s], plane(da, db))

    def got_m(ka, kb):
        got(("m", ka, kb), M.at[slot(ka, kb)])

    def send_t(k, hf, d):
        to = (k + (NZ - 1 if d == 0 else 1)) % NZ
        send(("t", to, hf), T.at[PLACE[k], hf], T.at[PLACE[to], hf], z_dev[d])

    def got_t(k, hf):
        got(("t", k, hf), T.at[PLACE[k], hf])

    def to_sib(k):
        send(("ts", k), T.at[PLACE[k]], T.at[NZ + PLACE[k]], sib)

    def got_sib(k):
        got(("ts", k), T.at[NZ + PLACE[k]])

    for step in (0, 1):
        for d in (0, 1):
            hf = d ^ step
            send_t(0, hf, d)
            send_u(0, 0, hf, 0, (1, 3)[d])
            send_u(0, 0, hf, (1, 3)[d], 0)
    for hf in (0, 1):
        send_u(0, 0, hf, 2, 0)
    for to in ((1, 0), (3, 0), (2, 0), (0, 1), (0, 3)):
        send_m(0, 0, *to)
    to_sib(0)

    tacc[...] = jnp.zeros_like(tacc)
    svec[...] = jnp.zeros_like(svec)

    def fwd_b(ka, d):
        hf = d
        kb = (3, 1)[d]
        got_u(ka, kb, hf)
        send_u(ka, kb, hf, 0, (1, 3)[d])

    def along_b(ka, hf):
        got_u(ka, 0, hf)
        for d in ((0, 1) if hf == 0 else (1, 0)):
            send_u(ka, 0, hf, 0, (1, 3)[d])

    def meta_b(ka):
        got_m(ka, 0)
        send_m(ka, 0, 0, 1)
        send_m(ka, 0, 0, 3)

    def rest_b(ka):
        got_u(ka, 3, 1)
        got_u(ka, 1, 0)
        got_m(ka, 3)
        send_m(ka, 3, 0, 1)
        got_m(ka, 1)

    def last_b(ka):
        got_u(ka, 2, 0)
        got_u(ka, 2, 1)
        got_m(ka, 2)

    got_t(7, 0)
    send_t(7, 0, 0)
    got_t(1, 1)
    send_t(1, 1, 1)
    fwd_b(0, 0)
    fwd_b(0, 1)
    along_b(3, 0)
    along_b(1, 1)
    got_t(7, 1)
    send_t(7, 1, 0)
    got_t(1, 0)
    send_t(1, 0, 1)
    along_b(3, 1)
    along_b(1, 0)
    to_sib(7)
    to_sib(1)
    along_b(2, 0)
    along_b(2, 1)
    meta_b(3)
    meta_b(1)
    meta_b(2)
    rest_b(0)
    got_t(6, 0)
    send_t(6, 0, 0)
    got_t(2, 1)
    send_t(2, 1, 1)
    for ka in (3, 1):
        fwd_b(ka, 0)
        fwd_b(ka, 1)
    got_t(6, 1)
    send_t(6, 1, 0)
    got_t(2, 0)
    send_t(2, 0, 1)
    to_sib(6)
    to_sib(2)

    base = yh * 1024 + (group // 2) * 128
    k1 = m * LOG2E
    k2 = shift0 * LOG2E

    def lane_vec(v, r):
        return M[2 * v, r:r + 1] + M[2 * v + 1, r:r + 1]

    def transpose_texts(q):
        flipped = T[4 * q:4 * q + 4].reshape(256, D).T
        Tt[:, :, q * 256:(q + 1) * 256] = flipped.reshape(8, FEAT, 256)

    def transpose_images(kb):
        b_ = (pb + kb) % SIDE
        flipped = U[pl.ds(b_ * SIDE, SIDE)].reshape(256, D).T
        for i in (0, 1):
            Ut[2 * b_ + i] = flipped[:, i * 128:(i + 1) * 128].reshape(8, FEAT, 128)

    def weights(part, kb):
        b_ = (pb + kb) % SIDE
        images = U[pl.ds(b_ * SIDE, SIDE)].reshape(256, D)
        label = jnp.concatenate([lane_vec(2 * b_, 1), lane_vec(2 * b_ + 1, 1)], axis=1)
        row = lax.broadcasted_iota(jnp.int32, (ROWS, 1), 0)
        for side in (0, 1):
            rows = T[pl.ds(side * NZ + part * 4, 4)].reshape(256, D)
            cos = lax.dot_general(rows, images, (((1,), (1,)), ((), ())), preferred_element_type=f32)
            owner = core if side == 0 else 1 - core
            ids = []
            for j in range(4):
                k = jnp.where(part == 0, ORDER[j], ORDER[4 + j])
                ids.append(row + ((z + k) % NZ * 2048 + base + owner * ROWS))
            match = jnp.concatenate(ids, axis=0).astype(f32) == label
            logit = cos * k1 + k2
            e = jnp.exp2(jnp.where(match, logit, -logit))
            w = (jnp.where(match, -m, m) / (1.0 + e)).astype(bf16)
            at_row = pl.ds(pl.multiple_of(side * 512 + part * 256, 256), 256)
            wc = w.astype(f32) * cos
            total = jnp.sum(wc, axis=0, keepdims=True)
            for i in (0, 1):
                cut = slice(i * 128, (i + 1) * 128)
                W[2 * b_ + i, at_row] = w[:, cut]
                svec[2 * b_ + i] += jnp.broadcast_to(total[:, cut], (8, 128))
            tacc[side * 2 + part] += wc[:, :128] + wc[:, 128:]

    for k in (0, 7, 1, 6):
        got_sib(k)
    weights(1, 0)
    got_t(5, 0)
    send(("t", 4, 0), T.at[PLACE[5], 0], T.at[PLACE[4], 0], z_dev[0])
    got_t(3, 1)
    send(("t", 4, 1), T.at[PLACE[3], 1], T.at[PLACE[4], 1], z_dev[1])
    fwd_b(2, 0)
    fwd_b(2, 1)
    got_t(5, 1)
    got_t(3, 0)
    to_sib(5)
    to_sib(3)
    for ka in (3, 1, 2):
        rest_b(ka)

    @pl.loop(0, 2)
    def _(i):
        weights(1, 1 + 2 * i)

    transpose_texts(1)
    transpose_texts(3)
    for kb in (0, 1, 3):
        transpose_images(kb)

    for ka in (0, 3, 1, 2):
        last_b(ka)
    got_t(4, 0)
    got_t(4, 1)
    to_sib(4)
    weights(1, 2)
    for k in (2, 5, 3, 4):
        got_sib(k)

    @pl.loop(0, 4)
    def _(i):
        weights(0, i)

    transpose_texts(0)
    transpose_texts(2)
    transpose_images(2)

    def text_part(q):
        lhs = jnp.concatenate([W[u, q * 256:(q + 1) * 256] for u in range(8)], axis=1)
        up = jnp.dot(lhs, U[...].reshape(1024, D), preferred_element_type=f32)
        along = jnp.sum(tacc[q], axis=1, keepdims=True)
        return (up - T[4 * q:4 * q + 4].reshape(256, D).astype(f32) * along).reshape(4, 2, HALF, D)

    def sib_part(part):
        sib_out[part] = text_part(2 + part).astype(bf16)
        send(("s", part), sib_out.at[part], sib_in.at[part], sib)

    def own_part(part):
        own[part] = text_part(part)

    def image_part(kb):
        b_ = (pb + kb) % SIDE

        @pl.loop(0, 2)
        def _(u):
            h = jnp.where(first, b_ // 2, u)
            units = [jnp.where(first, 4 * h + i, 2 * i + h) for i in range(4)]
            gs = [jnp.where(first, b_ % 2 * 4 + 2 * u + j, j * 4 + b_) for j in (0, 1)]
            lhs = jnp.concatenate([Tt[g] for g in gs], axis=0)
            rhs = jnp.concatenate([W[v] for v in units], axis=1)
            up = jnp.dot(lhs, rhs, preferred_element_type=f32)
            for hf in (0, 1):
                pair = units[2 * hf:2 * hf + 2]
                along = jnp.concatenate([svec[v][0:1] for v in pair], axis=1)
                inv = jnp.concatenate([lane_vec(v, 0) for v in pair], axis=1)
                for j, g in enumerate(gs):
                    unit = jnp.concatenate([Ut[v, g] for v in pair], axis=1).astype(f32)
                    part = up[j * FEAT:(j + 1) * FEAT, hf * 256:(hf + 1) * 256]
                    G[kb, 2 * u + j, hf] = ((part - unit * along) * inv).astype(bf16)

    A_ORDER = (2, 1, 3, 0)

    def a_at(ka):
        return (pa + ka) % SIDE

    def gb_far():
        for ka in A_ORDER:
            for d in (0, 1):
                send(("gh", ka, d), G.at[2, a_at(ka), d], rbh.at[ka, d], b_dev[d])

    def gb_near(d, fresh):
        kb = (1, 3)[d]
        for ka in A_ORDER:
            hf = 1 - d if fresh else d
            if not fresh:
                got(("gh", ka, d), rbh.at[ka, d])
                G[kb, a_at(ka), hf] = (G[kb, a_at(ka), hf].astype(f32) + rbh[ka, d].astype(f32)).astype(bf16)
            send(("gf", ka, d, hf), G.at[kb, a_at(ka), hf], rbf.at[ka, d, hf], b_dev[d])

    def gb_sum(ka):
        for d in (0, 1):
            for hf in (0, 1):
                got(("gf", ka, d, hf), rbf.at[ka, d, hf])
        return G[0, a_at(ka)].astype(f32) + rbf[ka, 0].astype(f32) + rbf[ka, 1].astype(f32)

    def text_sum(k, hf):
        p = PLACE[k]
        return own[p // 4, p % 4, hf] + sib_in[p // 4, p % 4, hf].astype(f32)

    def text_step(i, d, hf):
        k = (4 - i if d == 0 else 4 + i) % NZ
        value = text_sum(k, hf)
        if i > 1 or (i == 1 and hf == d):
            got(("r", d, i - 1, hf), trecv.at[d, i - 1, hf])
            value = value + trecv[d, i - 1, hf].astype(f32)
        tstage[d, i, hf] = value.astype(bf16)
        send(("r", d, i, hf), tstage.at[d, i, hf], trecv.at[d, i, hf], z_dev[d])

    image_part(2)
    gb_far()
    sib_part(0)
    own_part(0)
    got(("s", 0), sib_in.at[0])
    text_step(0, 0, 0)
    text_step(0, 1, 1)
    text_step(1, 0, 1)
    text_step(1, 1, 0)
    image_part(1)
    gb_near(0, True)
    image_part(3)
    gb_near(1, True)
    gb_near(0, False)
    gb_near(1, False)
    text_step(1, 0, 0)
    text_step(1, 1, 1)
    sib_part(1)
    text_step(2, 0, 1)
    own_part(1)
    got(("s", 1), sib_in.at[1])
    text_step(2, 1, 0)
    image_part(0)
    text_step(2, 0, 0)
    text_step(2, 1, 1)
    for ka in (2, 1, 3):
        r1[ka - 1] = gb_sum(ka).astype(bf16)
        send(("ga", ka), r1.at[ka - 1], ra.at[ka - 1], plane(ka, 0))
    text_step(3, 0, 1)
    text_step(3, 1, 0)
    text_step(3, 0, 0)
    text_step(3, 1, 1)
    total = gb_sum(0)
    for ka in (1, 3, 2):
        got(("ga", ka), ra.at[ka - 1])
        total = total + ra[ka - 1].astype(f32)
    for c in (0, 1):
        fin[c] = total[:, c * PART:(c + 1) * PART]
    send(("x",), fin.at[1 - core], fin_in, sib)

    for hf in (0, 1):
        value = text_sum(0, hf)
        for d in (0, 1):
            got(("r", d, 3, hf), trecv.at[d, 3, hf])
            value = value + trecv[d, 3, hf].astype(f32)
        txt_out[hf * HALF:(hf + 1) * HALF] = value * t_inv[hf * HALF:(hf + 1) * HALF]

    got(("x",), fin_in)
    mine = fin[core]
    other = fin_in[...]
    even = jnp.where(first, mine, other)
    odd = jnp.where(first, other, mine)
    blocks = []
    for g in range(8):
        for half, j in ((even, g), (odd, g % 4 * 2 + g // 4)):
            lo = (j % 4) * ROWS
            blocks.append(half[j // 4][:, lo:lo + ROWS])
    img_out[...] = jnp.concatenate(blocks, axis=1).astype(bf16)

    for copy in started:
        copy.wait_send()


def local(picture_embeds, caption_embeds, positive_caption_ids, logit_multiplier, logit_shift):
    vmem = pl.BlockSpec(memory_space=pltpu.VMEM)
    hbm = pl.BlockSpec(memory_space=pl.ANY)
    smem = pl.BlockSpec(memory_space=pltpu.SMEM)
    dma = pltpu.SemaphoreType.DMA
    scratch = [
        pltpu.VMEM((ROWS, D), bf16),
        pltpu.VMEM((ROWS, D), bf16),
        pltpu.VMEM((16, 2, HALF, D), bf16),
        pltpu.VMEM((16, 8, 128), f32),
        pltpu.VMEM((16, 2, HALF, D), bf16),
        pltpu.VMEM((8, 8, FEAT, 128), bf16),
        pltpu.VMEM((8, FEAT, 1024), bf16),
        pltpu.VMEM((8, 1024, 128), bf16),
        pltpu.VMEM((4, 256, 128), f32),
        pltpu.VMEM((8, 8, 128), f32),
        pltpu.VMEM((2, 4, 2, HALF, D), f32),
        pltpu.VMEM((2, 4, 2, HALF, D), bf16),
        pltpu.VMEM((2, 4, 2, HALF, D), bf16),
        pltpu.VMEM((2, 4, 2, HALF, D), bf16),
        pltpu.VMEM((2, 4, 2, HALF, D), bf16),
        pltpu.VMEM((4, 4, 2, FEAT, 256), bf16),
        pltpu.VMEM((4, 2, FEAT, 256), bf16),
        pltpu.VMEM((4, 2, 2, FEAT, 256), bf16),
        pltpu.VMEM((3, 2, FEAT, 256), bf16),
        pltpu.VMEM((3, 2, FEAT, 256), bf16),
        pltpu.VMEM((2, 2, PART, 256), f32),
        pltpu.VMEM((2, PART, 256), f32),
        dma((N_SEM,)), dma((N_SEM,)), dma((2,)),
    ]
    return pl.pallas_call(
        kernel,
        out_shape=(jax.ShapeDtypeStruct((PART, 1024), bf16), jax.ShapeDtypeStruct((ROWS, D), f32)),
        in_specs=[hbm, hbm, vmem, smem, smem],
        out_specs=(vmem, vmem),
        scratch_shapes=scratch,
        compiler_params=pltpu.CompilerParams(
            collective_id=0, has_side_effects=True, vmem_limit_bytes=VMEM_MIB * 2**20),
        cost_estimate=pl.CostEstimate(flops=7 * 10**9, bytes_accessed=10**6, transcendentals=2**20),
    )(picture_embeds, caption_embeds, positive_caption_ids.reshape(1, ROWS), logit_multiplier, logit_shift)


def solution(mesh):
    placed = (P(("batch", "group"), None), P(("batch", "group"), None), P(("batch", "group")), P(), P())
    return jax.shard_map(
        local, mesh=mesh, in_specs=placed,
        out_specs=(P("group", "batch"), P(("batch", "group"), None)), check_vma=False)
```

```python
import functools

import jax
import jax.numpy as jnp
from jax import lax
from jax.experimental import pallas as pl
from jax.experimental.pallas import tpu as pltpu
from jax.sharding import PartitionSpec as P

EPS = 1e-06
ROWS = 64
HALF = ROWS // 2
D = 1152
SIDE = 4
NZ = 8
FEAT = D // 8
PART = D // 16
PAD = 80
LOG2E = 1.4426950408889634
f32 = jnp.float32
bf16 = jnp.bfloat16


def rdma(src, dst, ssem, rsem, dev):
    return pltpu.make_async_remote_copy(
        src_ref=src, dst_ref=dst, send_sem=ssem, recv_sem=rsem,
        device_id=dev, device_id_type=pl.DeviceIdType.MESH)


def unit_rows(values):
    wide = values.astype(f32)
    inverse = lax.rsqrt(jnp.sum(wide * wide, axis=1, keepdims=True) + EPS)
    return wide * inverse, inverse
VMEM_MIB = 48

ORDER = (4, 3, 5, 2, 6, 1, 7, 0)
PLACE = {k: i for i, k in enumerate(ORDER)}
N_SEM = 160


def kernel(pic_hbm, cap_hbm, lab_hbm, mul, shift, img_out, txt_out,
           pic, cap, lab, U, M, T, Ut, Tt, W, tacc, svec, own, sib_out, sib_in,
           tstage, trecv, G, rbh, rbf, ra, ra_sib, r1, fin, ssem, rsem, lsem):
    batch = lax.axis_index("batch")
    group = lax.axis_index("group")
    z, yh = batch // 2, batch % 2
    core = group % 2
    x = (group // 2) % SIDE
    y = yh * 2 + group // (2 * SIDE)
    first = core == 0
    pa = jnp.where(first, x, y)
    pb = jnp.where(first, y, x)

    def dev(x_, y_, z_, c_):
        return (z_ * 2 + y_ // 2, ((y_ % 2) * SIDE + x_) * 2 + c_)

    def slot(ka, kb):
        return (pb + kb) % SIDE * SIDE + (pa + ka) % SIDE

    def plane(ka, kb, c_=core):
        a_ = (pa + ka) % SIDE
        b_ = (pb + kb) % SIDE
        return dev(jnp.where(first, a_, b_), jnp.where(first, b_, a_), z, c_)

    z_dev = (dev(x, y, (z + 1) % NZ, core), dev(x, y, (z + NZ - 1) % NZ, core))
    z_cross = (dev(x, y, (z + 1) % NZ, 1 - core), dev(x, y, (z + NZ - 1) % NZ, 1 - core))
    b_dev = (plane(0, 1), plane(0, SIDE - 1))
    sib = dev(x, y, z, 1 - core)

    loads = [pltpu.make_async_copy(src, dst, lsem.at[i]) for i, (src, dst) in enumerate(
        ((pic_hbm, pic), (cap_hbm, cap), (lab_hbm, lab)))]
    for load in loads:
        load.start()
    barrier = pltpu.get_barrier_semaphore()
    near = (*z_dev, *z_cross, *b_dev, plane(0, 2), plane(1, 0), plane(3, 0), plane(2, 0), sib)
    partners = (*near, *(plane(0, kb, 1 - core) for kb in (1, 2, 3)))
    for d in partners:
        pl.semaphore_signal(barrier, inc=1, device_id=d, device_id_type=pl.DeviceIdType.MESH)

    table = {}
    started = []

    def at(key):
        i = table.setdefault(key, len(table))
        assert i < N_SEM
        return i

    def send(key, src, dst, to):
        copy = rdma(src, dst, ssem.at[at(key)], rsem.at[at(key)], to)
        copy.start()
        started.append(copy)

    def got(key, dst):
        rdma(dst, dst, ssem.at[at(key)], rsem.at[at(key)], sib).wait_recv()

    me = slot(0, 0)
    loads[0].wait()
    p_unit, p_inv = unit_rows(pic[...])
    U[me] = p_unit.astype(bf16).reshape(2, HALF, D)

    def send_u(ka, kb, hf, da, db):
        s = slot(ka, kb)
        send(("u", (ka - da) % SIDE, (kb - db) % SIDE, hf), U.at[s, hf], U.at[s, hf], plane(da, db))

    def got_u(ka, kb, hf):
        got(("u", ka, kb, hf), U.at[slot(ka, kb), hf])

    def send_m(ka, kb, da, db):
        s = slot(ka, kb)
        send(("m", (ka - da) % SIDE, (kb - db) % SIDE), M.at[s], M.at[s], plane(da, db))

    def got_m(ka, kb):
        got(("m", ka, kb), M.at[slot(ka, kb)])

    def send_t(k, hf, d):
        to = (k + (NZ - 1 if d == 0 else 1)) % NZ
        send(("t", to, hf), T.at[PLACE[k], hf], T.at[PLACE[to], hf], z_dev[d])
        if to == NZ // 2:
            send(("tx", hf), T.at[PLACE[k], hf], T.at[NZ + PLACE[to], hf], z_cross[d])

    def got_t(k, hf):
        got(("t", k, hf), T.at[PLACE[k], hf])

    def got_t4():
        for hf in (0, 1):
            got_t(4, hf)
            got(("tx", hf), T.at[NZ + PLACE[4], hf])

    def to_sib(k):
        send(("ts", k), T.at[PLACE[k]], T.at[NZ + PLACE[k]], sib)

    def got_sib(k):
        got(("ts", k), T.at[NZ + PLACE[k]])

    pl.semaphore_wait(barrier, len(partners))
    for hf in (0, 1):
        send_u(0, 0, hf, 2, 0)
    loads[1].wait()
    t_unit, t_inv = unit_rows(cap[...])
    T[PLACE[0]] = t_unit.astype(bf16).reshape(2, HALF, D)
    for step in (0, 1):
        for d in (0, 1):
            send_t(0, d ^ step, d)
    for step in (0, 1):
        for d in (0, 1):
            send_u(0, 0, d ^ step, (1, 3)[d], 0)
    loads[2].wait()
    spread = jnp.broadcast_to(p_inv, (ROWS, 128))
    inv_lane = jnp.concatenate([spread, spread], axis=0).T[0:8]
    lab_row = lab[...].astype(f32)
    lab_lane = jnp.broadcast_to(jnp.concatenate([lab_row, lab_row], axis=1), (8, 128))
    row8 = lax.broadcasted_iota(jnp.int32, (8, 128), 0)
    lane8 = lax.broadcasted_iota(jnp.int32, (8, 128), 1)
    meta = jnp.where(row8 == 0, inv_lane, jnp.where(row8 == 1, lab_lane, 0.0))
    M[me] = jnp.where(lane8 // ROWS == pa % 2, meta, 0.0)
    for to in ((2, 0), (1, 0), (3, 0), (0, 2), (0, 1), (0, 3)):
        send_m(0, 0, *to)
    to_sib(0)
    for step in (0, 1):
        for d in (0, 1):
            send_u(0, 0, d ^ step, 0, (1, 3)[d])

    tacc[...] = jnp.zeros_like(tacc)
    svec[...] = jnp.zeros_like(svec)

    def fwd_b(ka, d):
        hf = d
        kb = (3, 1)[d]
        got_u(ka, kb, hf)
        send_u(ka, kb, hf, 0, (1, 3)[d])

    def along_b(ka, hf):
        got_u(ka, 0, hf)
        for d in ((0, 1) if hf == 0 else (1, 0)):
            send_u(ka, 0, hf, 0, (1, 3)[d])

    def meta_b(ka):
        got_m(ka, 0)
        for kb in (2, 1, 3):
            send_m(ka, 0, 0, kb)

    def row(kb):
        for ka in range(SIDE):
            if kb == 2:
                got_u(ka, 2, 0)
                got_u(ka, 2, 1)
            elif kb:
                got_u(ka, kb, 1 if kb == 3 else 0)
            if kb:
                got_m(ka, kb)

    m = mul[0]
    shift0 = shift[0]
    base = yh * 1024 + (group // 2) * 128
    k1 = m * LOG2E
    k2 = shift0 * LOG2E

    def lane_vec(v, r):
        return M[2 * v, r:r + 1] + M[2 * v + 1, r:r + 1]

    def transpose_texts(place, n):
        for side in (0, NZ):
            lo = (side + place) * ROWS
            flipped = T[side + place:side + place + n].reshape(n * ROWS, D).T
            Tt[:, :, lo:lo + n * ROWS] = flipped.reshape(8, FEAT, n * ROWS)

    def transpose_images(kb):
        b_ = (pb + kb) % SIDE
        flipped = U[pl.ds(b_ * SIDE, SIDE)].reshape(256, D).T
        for i in (0, 1):
            Ut[2 * b_ + i] = flipped[:, i * 128:(i + 1) * 128].reshape(8, FEAT, 128)

    def weights(place, n, kb):
        b_ = (pb + kb) % SIDE
        images = U[pl.ds(b_ * SIDE, SIDE)].reshape(256, D)
        label = jnp.concatenate([lane_vec(2 * b_, 1), lane_vec(2 * b_ + 1, 1)], axis=1)
        row = lax.broadcasted_iota(jnp.int32, (ROWS, 1), 0)
        size = n * ROWS
        for side in (0, 1):
            lo = (side * NZ + place) * ROWS
            rows = T[side * NZ + place:side * NZ + place + n].reshape(size, D)
            cos = lax.dot_general(rows, images, (((1,), (1,)), ((), ())), preferred_element_type=f32)
            owner = core if side == 0 else 1 - core
            ids = []
            for k in ORDER[place:place + n]:
                ids.append(row + ((z + k) % NZ * 2048 + base + owner * ROWS))
            match = jnp.concatenate(ids, axis=0).astype(f32) == label
            logit = cos * k1 + k2
            e = jnp.exp2(jnp.where(match, logit, -logit))
            w = (jnp.where(match, -m, m) / (1.0 + e)).astype(bf16)
            wc = w.astype(f32) * cos
            total = jnp.sum(wc, axis=0, keepdims=True)
            for i in (0, 1):
                cut = slice(i * 128, (i + 1) * 128)
                W[2 * b_ + i, lo:lo + size] = w[:, cut]
                svec[2 * b_ + i] += jnp.broadcast_to(total[:, cut], (8, 128))
            tacc[lo:lo + size] += wc[:, :128] + wc[:, 128:]

    along_b(2, 0)
    got_t(7, 0)
    send_t(7, 0, 0)
    got_t(1, 1)
    send_t(1, 1, 1)
    along_b(3, 0)
    along_b(1, 1)
    got_t(7, 1)
    send_t(7, 1, 0)
    got_t(1, 0)
    send_t(1, 0, 1)
    fwd_b(0, 0)
    fwd_b(0, 1)
    to_sib(7)
    to_sib(1)
    along_b(2, 1)
    meta_b(2)
    along_b(3, 1)
    along_b(1, 0)
    meta_b(1)
    meta_b(3)
    got_sib(1)
    got_sib(7)
    got_sib(0)
    row(0)
    weights(5, 3, 0)
    got_t(6, 0)
    send_t(6, 0, 0)
    got_t(2, 1)
    send_t(2, 1, 1)
    fwd_b(2, 0)
    transpose_texts(5, 3)
    transpose_images(0)
    fwd_b(3, 0)
    got_t(6, 1)
    send_t(6, 1, 0)
    got_t(2, 0)
    send_t(2, 0, 1)
    to_sib(6)
    fwd_b(1, 1)
    to_sib(2)
    got_sib(2)
    got_sib(6)
    weights(3, 2, 0)
    transpose_texts(3, 2)
    fwd_b(2, 1)
    got_t(5, 0)
    send_t(5, 0, 0)
    got_t(3, 1)
    send_t(3, 1, 1)
    fwd_b(3, 1)
    fwd_b(1, 0)
    row(1)
    got_t(5, 1)
    to_sib(5)
    got_t(3, 0)
    to_sib(3)
    row(3)
    weights(5, 3, 1)
    weights(5, 3, 3)
    weights(3, 2, 1)
    weights(3, 2, 3)
    transpose_images(1)
    transpose_images(3)
    row(2)
    weights(5, 3, 2)
    weights(3, 2, 2)
    transpose_images(2)
    got_t4()
    got_sib(3)
    got_sib(5)
    weights(0, 3, 0)
    weights(0, 3, 1)
    weights(0, 3, 2)
    weights(0, 3, 3)
    transpose_texts(0, 3)

    def text_part(place, n):
        rows = slice(place * ROWS, (place + n) * ROWS)
        lhs = jnp.concatenate([W[u, rows] for u in range(8)], axis=1)
        up = jnp.dot(lhs, U[...].reshape(1024, D), preferred_element_type=f32)
        along = jnp.sum(tacc[rows], axis=1, keepdims=True)
        unit = T[place:place + n].reshape(n * ROWS, D).astype(f32)
        return (up - unit * along).reshape(n, 2, HALF, D)

    def sib_part(place, n):
        cut = slice(place, place + n)
        sib_out[cut] = text_part(NZ + place, n).astype(bf16)
        send(("s", place), sib_out.at[cut], sib_in.at[cut], sib)

    def got_part(place, n):
        got(("s", place), sib_in.at[place:place + n])

    def own_part(place, n):
        own[place:place + n] = text_part(place, n)

    def image_part(kb, u):
        b_ = (pb + kb) % SIDE
        h = jnp.where(first, b_ // 2, u)
        units = [jnp.where(first, 4 * h + i, 2 * i + h) for i in range(4)]
        gs = [jnp.where(first, b_ % 2 * 4 + 2 * u + j, j * 4 + b_) for j in (0, 1)]
        lhs = jnp.concatenate([Tt[g] for g in gs], axis=0)
        rhs = jnp.concatenate([W[v] for v in units], axis=1)
        up = jnp.dot(lhs, rhs, preferred_element_type=f32)
        for hf in (0, 1):
            pair = units[2 * hf:2 * hf + 2]
            along = jnp.concatenate([svec[v][0:1] for v in pair], axis=1)
            inv = jnp.concatenate([lane_vec(v, 0) for v in pair], axis=1)
            for j, g in enumerate(gs):
                unit = jnp.concatenate([Ut[v, g] for v in pair], axis=1).astype(f32)
                part = up[j * FEAT:(j + 1) * FEAT, hf * 256:(hf + 1) * 256]
                G[kb, 2 * u + j, hf] = ((part - unit * along) * inv).astype(bf16)

    def a_at(ka):
        return (pa + ka) % SIDE

    def gb_far(ka):
        for d in (0, 1):
            send(("gh", ka, d), G.at[2, a_at(ka), d], rbh.at[ka, d], b_dev[d])

    def gb_near(d, ka, fresh):
        kb = (1, 3)[d]
        hf = 1 - d if fresh else d
        if not fresh:
            got(("gh", ka, d), rbh.at[ka, d])
            G[kb, a_at(ka), hf] = (G[kb, a_at(ka), hf].astype(f32) + rbh[ka, d].astype(f32)).astype(bf16)
        send(("gf", ka, d, hf), G.at[kb, a_at(ka), hf], rbf.at[ka, d, hf], b_dev[d])

    def gb_sum(ka):
        for d in (0, 1):
            for hf in (0, 1):
                got(("gf", ka, d, hf), rbf.at[ka, d, hf])
        return G[0, a_at(ka)].astype(f32) + rbf[ka, 0].astype(f32) + rbf[ka, 1].astype(f32)

    def text_sum(k, hf):
        p = PLACE[k]
        return own[p, hf] + sib_in[p, hf].astype(f32)

    def text_step(i, d, hf):
        k = (4 - i if d == 0 else 4 + i) % NZ
        value = text_sum(k, hf)
        if i > 1 or (i == 1 and hf == d):
            got(("r", d, i - 1, hf), trecv.at[d, i - 1, hf])
            value = value + trecv[d, i - 1, hf].astype(f32)
        tstage[d, i, hf] = value.astype(bf16)
        send(("r", d, i, hf), tstage.at[d, i, hf], trecv.at[d, i, hf], z_dev[d])

    def feature_halves(total, dst):
        for c in (0, 1):
            rows = jnp.concatenate([total[:, c * PART:(c + 1) * PART], jnp.zeros((2, PAD - PART, 256), f32)], axis=1)
            dst[c] = rows.astype(bf16)

    def along_a(ka):
        feature_halves(gb_sum(ka), r1.at[ka])
        i = at(("ga", 0, ka))
        at(("ga", 1, ka))
        for c in (0, 1):
            j = at(("ga to", c, ka))
            copy = rdma(r1.at[ka, c], ra.at[core, ka - 1], ssem.at[j], rsem.at[i + core], plane(ka, 0, c))
            copy.start()
            started.append(copy)

    def own_a():
        total = gb_sum(0)
        feature_halves(total, r1.at[0])
        for c in (0, 1):
            fin[c] = total[:, c * PART:(c + 1) * PART]
        send(("gs",), r1.at[0, 1 - core], ra_sib, sib)

    def image_end():
        got(("gs",), ra_sib)
        mine = fin[core]
        other = ra_sib[:, :PART].astype(f32)
        sums = [jnp.where(first, mine, other), jnp.where(first, other, mine)]
        for ka in (2, 1, 3):
            for c in (0, 1):
                got(("ga", c, ka), ra.at[c, ka - 1])
                sums[c] = sums[c] + ra[c, ka - 1, :, :PART].astype(f32)
        even, odd = sums
        blocks = []
        for g in range(8):
            for half, j in ((even, g), (odd, g % 4 * 2 + g // 4)):
                lo = (j % 4) * ROWS
                blocks.append(half[j // 4][:, lo:lo + ROWS])
        img_out[...] = jnp.concatenate(blocks, axis=1).astype(bf16)

    def text_end(hf):
        value = text_sum(0, hf)
        for d in (0, 1):
            got(("r", d, 3, hf), trecv.at[d, 3, hf])
            value = value + trecv[d, 3, hf].astype(f32)
        txt_out[hf * HALF:(hf + 1) * HALF] = value * t_inv[hf * HALF:(hf + 1) * HALF]

    u_far = (pa + 2) % SIDE // 2
    order = (2, 1, 3, 0)

    def image_parts(kb):
        @pl.loop(0, 2)
        def _(u):
            image_part(kb, u)

    image_part(2, u_far)
    gb_far(2)
    sib_part(0, 3)
    image_part(2, 1 - u_far)
    for ka in (1, 3, 0):
        gb_far(ka)
    own_part(0, 3)
    got_part(0, 3)
    text_step(0, 0, 0)
    text_step(0, 1, 1)
    text_step(1, 0, 1)
    text_step(1, 1, 0)
    image_parts(1)
    for ka in order:
        gb_near(0, ka, True)
    image_parts(3)
    for ka in order:
        gb_near(1, ka, True)
    for ka in order:
        for d in (0, 1):
            gb_near(d, ka, False)
    text_step(1, 0, 0)
    text_step(1, 1, 1)
    sib_part(3, 5)
    own_part(3, 5)
    got_part(3, 5)
    text_step(2, 0, 1)
    text_step(2, 1, 0)
    image_parts(0)
    text_step(2, 0, 0)
    text_step(2, 1, 1)
    for ka in (2, 1, 3):
        along_a(ka)
    text_step(3, 0, 1)
    text_step(3, 1, 0)
    own_a()
    text_step(3, 0, 0)
    text_step(3, 1, 1)
    image_end()
    text_end(0)
    text_end(1)

    for copy in started:
        copy.wait_send()


def local(picture_embeds, caption_embeds, positive_caption_ids, logit_multiplier, logit_shift):
    vmem = pl.BlockSpec(memory_space=pltpu.VMEM)
    hbm = pl.BlockSpec(memory_space=pltpu.HBM)
    smem = pl.BlockSpec(memory_space=pltpu.SMEM)
    dma = pltpu.SemaphoreType.DMA
    scratch = [
        pltpu.VMEM((ROWS, D), bf16),
        pltpu.VMEM((ROWS, D), bf16),
        pltpu.VMEM((1, ROWS), jnp.int32),
        pltpu.VMEM((16, 2, HALF, D), bf16),
        pltpu.VMEM((16, 8, 128), f32),
        pltpu.VMEM((16, 2, HALF, D), bf16),
        pltpu.VMEM((8, 8, FEAT, 128), bf16),
        pltpu.VMEM((8, FEAT, 1024), bf16),
        pltpu.VMEM((8, 1024, 128), bf16),
        pltpu.VMEM((1024, 128), f32),
        pltpu.VMEM((8, 8, 128), f32),
        pltpu.VMEM((NZ, 2, HALF, D), f32),
        pltpu.VMEM((NZ, 2, HALF, D), bf16),
        pltpu.VMEM((NZ, 2, HALF, D), bf16),
        pltpu.VMEM((2, 4, 2, HALF, D), bf16),
        pltpu.VMEM((2, 4, 2, HALF, D), bf16),
        pltpu.VMEM((4, 4, 2, FEAT, 256), bf16),
        pltpu.VMEM((4, 2, FEAT, 256), bf16),
        pltpu.VMEM((4, 2, 2, FEAT, 256), bf16),
        pltpu.VMEM((2, 3, 2, PAD, 256), bf16),
        pltpu.VMEM((2, PAD, 256), bf16),
        pltpu.VMEM((4, 2, 2, PAD, 256), bf16),
        pltpu.VMEM((2, 2, PART, 256), f32),
        dma((N_SEM,)), dma((N_SEM,)), dma((3,)),
    ]
    return pl.pallas_call(
        kernel,
        out_shape=(jax.ShapeDtypeStruct((PART, 1024), bf16), jax.ShapeDtypeStruct((ROWS, D), f32)),
        in_specs=[hbm, hbm, hbm, smem, smem],
        out_specs=(vmem, vmem),
        scratch_shapes=scratch,
        compiler_params=pltpu.CompilerParams(
            collective_id=0, has_side_effects=True, vmem_limit_bytes=VMEM_MIB * 2**20),
        cost_estimate=pl.CostEstimate(flops=7 * 10**9, bytes_accessed=10**6, transcendentals=2**20),
    )(*(pltpu.with_memory_space_constraint(v, pltpu.HBM) for v in (
        picture_embeds, caption_embeds, positive_caption_ids.reshape(1, ROWS))), logit_multiplier, logit_shift)


def solution(mesh):
    placed = (P(("batch", "group"), None), P(("batch", "group"), None), P(("batch", "group")), P(), P())
    return jax.shard_map(
        local, mesh=mesh, in_specs=placed,
        out_specs=(P("group", "batch"), P(("batch", "group"), None)), check_vma=False)
```

```python
import functools

import jax
import jax.numpy as jnp
from jax import lax
from jax.experimental import pallas as pl
from jax.experimental.pallas import tpu as pltpu
from jax.sharding import PartitionSpec as P

EPS = 1e-06
ROWS = 64
HALF = ROWS // 2
D = 1152
SIDE = 4
NZ = 8
FEAT = D // 8
PART = D // 16
PAD = 80
LOG2E = 1.4426950408889634
f32 = jnp.float32
bf16 = jnp.bfloat16


def rdma(src, dst, ssem, rsem, dev):
    return pltpu.make_async_remote_copy(
        src_ref=src, dst_ref=dst, send_sem=ssem, recv_sem=rsem,
        device_id=dev, device_id_type=pl.DeviceIdType.MESH)


def unit_rows(values):
    wide = values.astype(f32)
    inverse = lax.rsqrt(jnp.sum(wide * wide, axis=1, keepdims=True) + EPS)
    return wide * inverse, inverse
VMEM_MIB = 48

ORDER = (4, 3, 5, 2, 6, 1, 7, 0)
PLACE = {k: i for i, k in enumerate(ORDER)}
N_SEM = 160


def kernel(pic_hbm, cap_hbm, lab_hbm, mul, shift, img_out, txt_out,
           pic, cap, lab, U, M, T, Ut, Tt, W, tacc, svec, own, sib_out, sib_in,
           tstage, trecv, G, rbh, rbf, ra, ra_sib, r1, fin, ssem, rsem, lsem):
    batch = lax.axis_index("batch")
    group = lax.axis_index("group")
    z, yh = batch // 2, batch % 2
    core = group % 2
    x = (group // 2) % SIDE
    y = yh * 2 + group // (2 * SIDE)
    first = core == 0
    pa = jnp.where(first, x, y)
    pb = jnp.where(first, y, x)

    def dev(x_, y_, z_, c_):
        return (z_ * 2 + y_ // 2, ((y_ % 2) * SIDE + x_) * 2 + c_)

    def slot(ka, kb):
        return (pb + kb) % SIDE * SIDE + (pa + ka) % SIDE

    def plane(ka, kb, c_=core):
        a_ = (pa + ka) % SIDE
        b_ = (pb + kb) % SIDE
        return dev(jnp.where(first, a_, b_), jnp.where(first, b_, a_), z, c_)

    z_dev = (dev(x, y, (z + 1) % NZ, core), dev(x, y, (z + NZ - 1) % NZ, core))
    z_cross = (dev(x, y, (z + 1) % NZ, 1 - core), dev(x, y, (z + NZ - 1) % NZ, 1 - core))
    b_dev = (plane(0, 1), plane(0, SIDE - 1))
    sib = dev(x, y, z, 1 - core)

    loads = [pltpu.make_async_copy(src, dst, lsem.at[i]) for i, (src, dst) in enumerate(
        ((pic_hbm, pic), (cap_hbm, cap), (lab_hbm, lab)))]
    for load in loads:
        load.start()
    barrier = pltpu.get_barrier_semaphore()
    near = (*z_dev, *z_cross, *b_dev, plane(0, 2), plane(1, 0), plane(3, 0), plane(2, 0), sib)
    partners = (*near, *(plane(0, kb, 1 - core) for kb in (1, 2, 3)))
    for d in partners:
        pl.semaphore_signal(barrier, inc=1, device_id=d, device_id_type=pl.DeviceIdType.MESH)

    table = {}
    started = []

    def at(key):
        i = table.setdefault(key, len(table))
        assert i < N_SEM
        return i

    def send(key, src, dst, to):
        copy = rdma(src, dst, ssem.at[at(key)], rsem.at[at(key)], to)
        copy.start()
        started.append(copy)

    def got(key, dst):
        rdma(dst, dst, ssem.at[at(key)], rsem.at[at(key)], sib).wait_recv()

    me = slot(0, 0)
    loads[1].wait()
    t_unit, t_inv = unit_rows(cap[...])
    T[PLACE[0]] = t_unit.astype(bf16).reshape(2, HALF, D)
    loads[0].wait()
    p_unit, p_inv = unit_rows(pic[...])
    U[me] = p_unit.astype(bf16).reshape(2, HALF, D)
    pl.semaphore_wait(barrier, len(partners))
    def send_u(ka, kb, hf, da, db):
        s = slot(ka, kb)
        send(("u", (ka - da) % SIDE, (kb - db) % SIDE, hf), U.at[s, hf], U.at[s, hf], plane(da, db))

    def got_u(ka, kb, hf):
        got(("u", ka, kb, hf), U.at[slot(ka, kb), hf])

    def send_m(ka, kb, da, db):
        s = slot(ka, kb)
        send(("m", (ka - da) % SIDE, (kb - db) % SIDE), M.at[s], M.at[s], plane(da, db))

    def got_m(ka, kb):
        got(("m", ka, kb), M.at[slot(ka, kb)])

    def send_t(k, hf, d):
        to = (k + (NZ - 1 if d == 0 else 1)) % NZ
        send(("t", to, hf), T.at[PLACE[k], hf], T.at[PLACE[to], hf], z_dev[d])
        if to == NZ // 2:
            send(("tx", hf), T.at[PLACE[k], hf], T.at[NZ + PLACE[to], hf], z_cross[d])

    def got_t(k, hf):
        got(("t", k, hf), T.at[PLACE[k], hf])

    def got_t4():
        for hf in (0, 1):
            got_t(4, hf)
            got(("tx", hf), T.at[NZ + PLACE[4], hf])

    def to_sib(k):
        send(("ts", k), T.at[PLACE[k]], T.at[NZ + PLACE[k]], sib)

    def got_sib(k):
        got(("ts", k), T.at[NZ + PLACE[k]])

    for step in (0, 1):
        for d in (0, 1):
            send_t(0, d ^ step, d)
    for hf in (0, 1):
        send_u(0, 0, hf, 2, 0)
    for step in (0, 1):
        for d in (0, 1):
            send_u(0, 0, d ^ step, (1, 3)[d], 0)
    loads[2].wait()
    spread = jnp.broadcast_to(p_inv, (ROWS, 128))
    inv_lane = jnp.concatenate([spread, spread], axis=0).T[0:8]
    lab_row = lab[...].astype(f32)
    lab_lane = jnp.broadcast_to(jnp.concatenate([lab_row, lab_row], axis=1), (8, 128))
    row8 = lax.broadcasted_iota(jnp.int32, (8, 128), 0)
    lane8 = lax.broadcasted_iota(jnp.int32, (8, 128), 1)
    meta = jnp.where(row8 == 0, inv_lane, jnp.where(row8 == 1, lab_lane, 0.0))
    M[me] = jnp.where(lane8 // ROWS == pa % 2, meta, 0.0)
    for to in ((2, 0), (1, 0), (3, 0), (0, 2), (0, 1), (0, 3)):
        send_m(0, 0, *to)
    to_sib(0)
    for step in (0, 1):
        for d in (0, 1):
            send_u(0, 0, d ^ step, 0, (1, 3)[d])

    tacc[...] = jnp.zeros_like(tacc)
    svec[...] = jnp.zeros_like(svec)

    def fwd_b(ka, d):
        hf = d
        kb = (3, 1)[d]
        got_u(ka, kb, hf)
        send_u(ka, kb, hf, 0, (1, 3)[d])

    def along_b(ka, hf):
        got_u(ka, 0, hf)
        for d in ((0, 1) if hf == 0 else (1, 0)):
            send_u(ka, 0, hf, 0, (1, 3)[d])

    def meta_b(ka):
        got_m(ka, 0)
        for kb in (2, 1, 3):
            send_m(ka, 0, 0, kb)

    def row(kb):
        for ka in range(SIDE):
            if kb == 2:
                got_u(ka, 2, 0)
                got_u(ka, 2, 1)
            elif kb:
                got_u(ka, kb, 1 if kb == 3 else 0)
            if kb:
                got_m(ka, kb)

    m = mul[0]
    shift0 = shift[0]
    base = yh * 1024 + (group // 2) * 128
    k1 = m * LOG2E
    k2 = shift0 * LOG2E

    def lane_vec(v, r):
        return M[2 * v, r:r + 1] + M[2 * v + 1, r:r + 1]

    def transpose_texts(place, n):
        for side in (0, NZ):
            lo = (side + place) * ROWS
            flipped = T[side + place:side + place + n].reshape(n * ROWS, D).T
            Tt[:, :, lo:lo + n * ROWS] = flipped.reshape(8, FEAT, n * ROWS)

    def transpose_images(kb):
        b_ = (pb + kb) % SIDE
        flipped = U[pl.ds(b_ * SIDE, SIDE)].reshape(256, D).T
        for i in (0, 1):
            Ut[2 * b_ + i] = flipped[:, i * 128:(i + 1) * 128].reshape(8, FEAT, 128)

    def weights(place, n, kb):
        b_ = (pb + kb) % SIDE
        images = U[pl.ds(b_ * SIDE, SIDE)].reshape(256, D)
        label = jnp.concatenate([lane_vec(2 * b_, 1), lane_vec(2 * b_ + 1, 1)], axis=1)
        row = lax.broadcasted_iota(jnp.int32, (ROWS, 1), 0)
        size = n * ROWS
        for side in (0, 1):
            lo = (side * NZ + place) * ROWS
            rows = T[side * NZ + place:side * NZ + place + n].reshape(size, D)
            cos = lax.dot_general(rows, images, (((1,), (1,)), ((), ())), preferred_element_type=f32)
            owner = core if side == 0 else 1 - core
            ids = []
            for k in ORDER[place:place + n]:
                ids.append(row + ((z + k) % NZ * 2048 + base + owner * ROWS))
            match = jnp.concatenate(ids, axis=0).astype(f32) == label
            logit = cos * k1 + k2
            e = jnp.exp2(jnp.where(match, logit, -logit))
            w = (jnp.where(match, -m, m) / (1.0 + e)).astype(bf16)
            wc = w.astype(f32) * cos
            total = jnp.sum(wc, axis=0, keepdims=True)
            for i in (0, 1):
                cut = slice(i * 128, (i + 1) * 128)
                W[2 * b_ + i, lo:lo + size] = w[:, cut]
                svec[2 * b_ + i] += jnp.broadcast_to(total[:, cut], (8, 128))
            tacc[lo:lo + size] += wc[:, :128] + wc[:, 128:]

    got_t(7, 0)
    send_t(7, 0, 0)
    got_t(1, 1)
    send_t(1, 1, 1)
    got_t(7, 1)
    send_t(7, 1, 0)
    got_t(1, 0)
    send_t(1, 0, 1)
    to_sib(7)
    to_sib(1)
    along_b(3, 0)
    along_b(1, 1)
    along_b(2, 0)
    along_b(2, 1)
    fwd_b(0, 0)
    fwd_b(0, 1)
    along_b(3, 1)
    along_b(1, 0)
    meta_b(2)
    meta_b(1)
    meta_b(3)
    got_t(6, 0)
    send_t(6, 0, 0)
    got_t(2, 1)
    send_t(2, 1, 1)
    got_t(6, 1)
    send_t(6, 1, 0)
    got_t(2, 0)
    send_t(2, 0, 1)
    to_sib(6)
    to_sib(2)
    got_sib(1)
    got_sib(7)
    got_sib(0)
    row(0)
    weights(5, 3, 0)
    fwd_b(2, 0)
    fwd_b(2, 1)
    fwd_b(3, 0)
    fwd_b(1, 1)
    got_t(5, 0)
    send_t(5, 0, 0)
    got_t(3, 1)
    send_t(3, 1, 1)
    fwd_b(3, 1)
    fwd_b(1, 0)
    got_sib(2)
    got_sib(6)
    weights(3, 2, 0)
    got_t(5, 1)
    to_sib(5)
    got_t(3, 0)
    to_sib(3)
    transpose_texts(5, 3)
    transpose_texts(3, 2)
    transpose_images(0)
    row(1)
    row(3)
    weights(5, 3, 1)
    weights(5, 3, 3)
    weights(3, 2, 1)
    weights(3, 2, 3)
    transpose_images(1)
    transpose_images(3)
    got_t4()
    got_sib(3)
    got_sib(5)
    weights(0, 3, 0)
    weights(0, 3, 1)
    weights(0, 3, 3)
    transpose_texts(0, 3)
    row(2)
    weights(0, 8, 2)
    transpose_images(2)

    def text_part(place, n):
        rows = slice(place * ROWS, (place + n) * ROWS)
        lhs = jnp.concatenate([W[u, rows] for u in range(8)], axis=1)
        up = jnp.dot(lhs, U[...].reshape(1024, D), preferred_element_type=f32)
        along = jnp.sum(tacc[rows], axis=1, keepdims=True)
        unit = T[place:place + n].reshape(n * ROWS, D).astype(f32)
        return (up - unit * along).reshape(n, 2, HALF, D)

    def sib_part(place, n):
        cut = slice(place, place + n)
        sib_out[cut] = text_part(NZ + place, n).astype(bf16)
        send(("s", place), sib_out.at[cut], sib_in.at[cut], sib)

    def got_part(place, n):
        got(("s", place), sib_in.at[place:place + n])

    def own_part(place, n):
        own[place:place + n] = text_part(place, n)

    def image_part(kb, u):
        b_ = (pb + kb) % SIDE
        h = jnp.where(first, b_ // 2, u)
        units = [jnp.where(first, 4 * h + i, 2 * i + h) for i in range(4)]
        gs = [jnp.where(first, b_ % 2 * 4 + 2 * u + j, j * 4 + b_) for j in (0, 1)]
        lhs = jnp.concatenate([Tt[g] for g in gs], axis=0)
        rhs = jnp.concatenate([W[v] for v in units], axis=1)
        up = jnp.dot(lhs, rhs, preferred_element_type=f32)
        for hf in (0, 1):
            pair = units[2 * hf:2 * hf + 2]
            along = jnp.concatenate([svec[v][0:1] for v in pair], axis=1)
            inv = jnp.concatenate([lane_vec(v, 0) for v in pair], axis=1)
            for j, g in enumerate(gs):
                unit = jnp.concatenate([Ut[v, g] for v in pair], axis=1).astype(f32)
                part = up[j * FEAT:(j + 1) * FEAT, hf * 256:(hf + 1) * 256]
                G[kb, 2 * u + j, hf] = ((part - unit * along) * inv).astype(bf16)

    def a_at(ka):
        return (pa + ka) % SIDE

    def gb_far(ka):
        for d in (0, 1):
            send(("gh", ka, d), G.at[2, a_at(ka), d], rbh.at[ka, d], b_dev[d])

    def gb_near(d, ka, fresh):
        kb = (1, 3)[d]
        hf = 1 - d if fresh else d
        if not fresh:
            got(("gh", ka, d), rbh.at[ka, d])
            G[kb, a_at(ka), hf] = (G[kb, a_at(ka), hf].astype(f32) + rbh[ka, d].astype(f32)).astype(bf16)
        send(("gf", ka, d, hf), G.at[kb, a_at(ka), hf], rbf.at[ka, d, hf], b_dev[d])

    def gb_sum(ka):
        for d in (0, 1):
            for hf in (0, 1):
                got(("gf", ka, d, hf), rbf.at[ka, d, hf])
        return G[0, a_at(ka)].astype(f32) + rbf[ka, 0].astype(f32) + rbf[ka, 1].astype(f32)

    def text_sum(k, hf):
        p = PLACE[k]
        return own[p, hf] + sib_in[p, hf].astype(f32)

    def text_step(i, d, hf):
        k = (4 - i if d == 0 else 4 + i) % NZ
        value = text_sum(k, hf)
        if i > 1 or (i == 1 and hf == d):
            got(("r", d, i - 1, hf), trecv.at[d, i - 1, hf])
            value = value + trecv[d, i - 1, hf].astype(f32)
        tstage[d, i, hf] = value.astype(bf16)
        send(("r", d, i, hf), tstage.at[d, i, hf], trecv.at[d, i, hf], z_dev[d])

    def feature_halves(total, dst):
        for c in (0, 1):
            rows = jnp.concatenate([total[:, c * PART:(c + 1) * PART], jnp.zeros((2, PAD - PART, 256), f32)], axis=1)
            dst[c] = rows.astype(bf16)

    def along_a(ka):
        feature_halves(gb_sum(ka), r1.at[ka])
        i = at(("ga", 0, ka))
        at(("ga", 1, ka))
        for c in (0, 1):
            j = at(("ga to", c, ka))
            copy = rdma(r1.at[ka, c], ra.at[core, ka - 1], ssem.at[j], rsem.at[i + core], plane(ka, 0, c))
            copy.start()
            started.append(copy)

    def own_a():
        total = gb_sum(0)
        feature_halves(total, r1.at[0])
        for c in (0, 1):
            fin[c] = total[:, c * PART:(c + 1) * PART]
        send(("gs",), r1.at[0, 1 - core], ra_sib, sib)

    def image_end():
        got(("gs",), ra_sib)
        mine = fin[core]
        other = ra_sib[:, :PART].astype(f32)
        sums = [jnp.where(first, mine, other), jnp.where(first, other, mine)]
        for ka in (2, 1, 3):
            for c in (0, 1):
                got(("ga", c, ka), ra.at[c, ka - 1])
                sums[c] = sums[c] + ra[c, ka - 1, :, :PART].astype(f32)
        even, odd = sums
        blocks = []
        for g in range(8):
            for half, j in ((even, g), (odd, g % 4 * 2 + g // 4)):
                lo = (j % 4) * ROWS
                blocks.append(half[j // 4][:, lo:lo + ROWS])
        img_out[...] = jnp.concatenate(blocks, axis=1).astype(bf16)

    def text_end(hf):
        value = text_sum(0, hf)
        for d in (0, 1):
            got(("r", d, 3, hf), trecv.at[d, 3, hf])
            value = value + trecv[d, 3, hf].astype(f32)
        txt_out[hf * HALF:(hf + 1) * HALF] = value * t_inv[hf * HALF:(hf + 1) * HALF]

    u_far = (pa + 2) % SIDE // 2
    order = (2, 1, 3, 0)

    def image_parts(kb):
        @pl.loop(0, 2)
        def _(u):
            image_part(kb, u)

    image_part(2, u_far)
    gb_far(2)
    image_part(2, 1 - u_far)
    for ka in (1, 3, 0):
        gb_far(ka)
    sib_part(0, 3)
    own_part(0, 3)
    got_part(0, 3)
    text_step(0, 0, 0)
    text_step(0, 1, 1)
    text_step(1, 0, 1)
    text_step(1, 1, 0)
    image_parts(1)
    for ka in order:
        gb_near(0, ka, True)
    image_parts(3)
    for ka in order:
        gb_near(1, ka, True)
    for ka in order:
        for d in (0, 1):
            gb_near(d, ka, False)
    text_step(1, 0, 0)
    text_step(1, 1, 1)
    sib_part(3, 5)
    own_part(3, 5)
    got_part(3, 5)
    text_step(2, 0, 1)
    text_step(2, 1, 0)
    image_parts(0)
    text_step(2, 0, 0)
    text_step(2, 1, 1)
    for ka in (2, 1, 3):
        along_a(ka)
    text_step(3, 0, 1)
    text_step(3, 1, 0)
    own_a()
    text_step(3, 0, 0)
    text_step(3, 1, 1)
    image_end()
    text_end(0)
    text_end(1)

    for copy in started:
        copy.wait_send()


def local(picture_embeds, caption_embeds, positive_caption_ids, logit_multiplier, logit_shift):
    vmem = pl.BlockSpec(memory_space=pltpu.VMEM)
    hbm = pl.BlockSpec(memory_space=pltpu.HBM)
    smem = pl.BlockSpec(memory_space=pltpu.SMEM)
    dma = pltpu.SemaphoreType.DMA
    scratch = [
        pltpu.VMEM((ROWS, D), bf16),
        pltpu.VMEM((ROWS, D), bf16),
        pltpu.VMEM((1, ROWS), jnp.int32),
        pltpu.VMEM((16, 2, HALF, D), bf16),
        pltpu.VMEM((16, 8, 128), f32),
        pltpu.VMEM((16, 2, HALF, D), bf16),
        pltpu.VMEM((8, 8, FEAT, 128), bf16),
        pltpu.VMEM((8, FEAT, 1024), bf16),
        pltpu.VMEM((8, 1024, 128), bf16),
        pltpu.VMEM((1024, 128), f32),
        pltpu.VMEM((8, 8, 128), f32),
        pltpu.VMEM((NZ, 2, HALF, D), f32),
        pltpu.VMEM((NZ, 2, HALF, D), bf16),
        pltpu.VMEM((NZ, 2, HALF, D), bf16),
        pltpu.VMEM((2, 4, 2, HALF, D), bf16),
        pltpu.VMEM((2, 4, 2, HALF, D), bf16),
        pltpu.VMEM((4, 4, 2, FEAT, 256), bf16),
        pltpu.VMEM((4, 2, FEAT, 256), bf16),
        pltpu.VMEM((4, 2, 2, FEAT, 256), bf16),
        pltpu.VMEM((2, 3, 2, PAD, 256), bf16),
        pltpu.VMEM((2, PAD, 256), bf16),
        pltpu.VMEM((4, 2, 2, PAD, 256), bf16),
        pltpu.VMEM((2, 2, PART, 256), f32),
        dma((N_SEM,)), dma((N_SEM,)), dma((3,)),
    ]
    return pl.pallas_call(
        kernel,
        out_shape=(jax.ShapeDtypeStruct((PART, 1024), bf16), jax.ShapeDtypeStruct((ROWS, D), f32)),
        in_specs=[hbm, hbm, hbm, smem, smem],
        out_specs=(vmem, vmem),
        scratch_shapes=scratch,
        compiler_params=pltpu.CompilerParams(
            collective_id=0, has_side_effects=True, vmem_limit_bytes=VMEM_MIB * 2**20),
        cost_estimate=pl.CostEstimate(flops=7 * 10**9, bytes_accessed=10**6, transcendentals=2**20),
    )(*(pltpu.with_memory_space_constraint(v, pltpu.HBM) for v in (
        picture_embeds, caption_embeds, positive_caption_ids.reshape(1, ROWS))), logit_multiplier, logit_shift)


def solution(mesh):
    placed = (P(("batch", "group"), None), P(("batch", "group"), None), P(("batch", "group")), P(), P())
    return jax.shard_map(
        local, mesh=mesh, in_specs=placed,
        out_specs=(P("group", "batch"), P(("batch", "group"), None)), check_vma=False)
```

```python
import functools

import jax
import jax.numpy as jnp
from jax import lax
from jax.experimental import pallas as pl
from jax.experimental.pallas import tpu as pltpu
from jax.sharding import PartitionSpec as P

EPS = 1e-06
ROWS = 64
HALF = ROWS // 2
D = 1152
SIDE = 4
NZ = 8
FEAT = D // 8
PART = D // 16
PAD = 80
LOG2E = 1.4426950408889634
f32 = jnp.float32
bf16 = jnp.bfloat16


def rdma(src, dst, ssem, rsem, dev):
    return pltpu.make_async_remote_copy(
        src_ref=src, dst_ref=dst, send_sem=ssem, recv_sem=rsem,
        device_id=dev, device_id_type=pl.DeviceIdType.MESH)


def unit_rows(values):
    wide = values.astype(f32)
    inverse = lax.rsqrt(jnp.sum(wide * wide, axis=1, keepdims=True) + EPS)
    return wide * inverse, inverse
VMEM_MIB = 48

ORDER = (4, 3, 5, 2, 6, 1, 7, 0)
PLACE = {k: i for i, k in enumerate(ORDER)}
N_SEM = 160


def kernel(pic_hbm, cap_hbm, lab_hbm, mul, shift, img_out, txt_out,
           pic, cap, lab, U, M, T, Ut, Tt, W, tacc, svec, own, sib_out, sib_in,
           tstage, trecv, G, rbh, rbf, rbn, ra, ra_sib, r1, fin, ssem, rsem, lsem):
    batch = lax.axis_index("batch")
    group = lax.axis_index("group")
    z, yh = batch // 2, batch % 2
    core = group % 2
    x = (group // 2) % SIDE
    y = yh * 2 + group // (2 * SIDE)
    first = core == 0
    pa = jnp.where(first, x, y)
    pb = jnp.where(first, y, x)

    def dev(x_, y_, z_, c_):
        return (z_ * 2 + y_ // 2, ((y_ % 2) * SIDE + x_) * 2 + c_)

    def slot(ka, kb):
        return (pb + kb) % SIDE * SIDE + (pa + ka) % SIDE

    def plane(ka, kb, c_=core):
        a_ = (pa + ka) % SIDE
        b_ = (pb + kb) % SIDE
        return dev(jnp.where(first, a_, b_), jnp.where(first, b_, a_), z, c_)

    z_dev = (dev(x, y, (z + 1) % NZ, core), dev(x, y, (z + NZ - 1) % NZ, core))
    z_cross = (dev(x, y, (z + 1) % NZ, 1 - core), dev(x, y, (z + NZ - 1) % NZ, 1 - core))
    b_dev = (plane(0, 1), plane(0, SIDE - 1))
    sib = dev(x, y, z, 1 - core)

    loads = [pltpu.make_async_copy(src, dst, lsem.at[i]) for i, (src, dst) in enumerate(
        ((cap_hbm, cap), (pic_hbm, pic), (lab_hbm, lab)))]
    for load in loads:
        load.start()
    barrier = pltpu.get_barrier_semaphore()
    near = (*z_dev, *z_cross, *b_dev, plane(0, 2), plane(1, 0), plane(3, 0), plane(2, 0), sib)
    partners = (*near, *(plane(0, kb, 1 - core) for kb in (1, 2, 3)))
    for d in partners:
        pl.semaphore_signal(barrier, inc=1, device_id=d, device_id_type=pl.DeviceIdType.MESH)

    table = {}
    started = []

    def at(key):
        i = table.setdefault(key, len(table))
        assert i < N_SEM
        return i

    def send(key, src, dst, to):
        copy = rdma(src, dst, ssem.at[at(key)], rsem.at[at(key)], to)
        copy.start()
        started.append(copy)

    def got(key, dst):
        rdma(dst, dst, ssem.at[at(key)], rsem.at[at(key)], sib).wait_recv()

    me = slot(0, 0)
    loads[0].wait()
    t_unit, t_inv = unit_rows(cap[...])
    T[PLACE[0]] = t_unit.astype(bf16).reshape(2, HALF, D)
    loads[1].wait()
    p_unit, p_inv = unit_rows(pic[...])
    U[me] = p_unit.astype(bf16).reshape(2, HALF, D)
    pl.semaphore_wait(barrier, len(partners))
    def send_u(ka, kb, hf, da, db):
        s = slot(ka, kb)
        send(("u", (ka - da) % SIDE, (kb - db) % SIDE, hf), U.at[s, hf], U.at[s, hf], plane(da, db))

    def got_u(ka, kb, hf):
        got(("u", ka, kb, hf), U.at[slot(ka, kb), hf])

    def send_m(ka):
        send(("m", SIDE - ka), M.at[me], M.at[me], plane(ka, 0))

    def line(kb):
        return M.at[pl.ds((pb + kb) % SIDE * SIDE, SIDE)]

    def send_t(k, hf, d):
        to = (k + (NZ - 1 if d == 0 else 1)) % NZ
        send(("t", to, hf), T.at[PLACE[k], hf], T.at[PLACE[to], hf], z_dev[d])
        if to == NZ // 2:
            send(("tx", hf), T.at[PLACE[k], hf], T.at[NZ + PLACE[to], hf], z_cross[d])

    def got_t(k, hf):
        got(("t", k, hf), T.at[PLACE[k], hf])

    def got_t4():
        for hf in (0, 1):
            got_t(4, hf)
            got(("tx", hf), T.at[NZ + PLACE[4], hf])

    def to_sib(k):
        send(("ts", k), T.at[PLACE[k]], T.at[NZ + PLACE[k]], sib)

    def got_sib(k):
        got(("ts", k), T.at[NZ + PLACE[k]])

    for step in (0, 1):
        for d in (0, 1):
            send_t(0, d ^ step, d)
    for hf in (0, 1):
        send_u(0, 0, hf, 2, 0)
    for step in (0, 1):
        for d in (0, 1):
            send_u(0, 0, d ^ step, (1, 3)[d], 0)
    loads[2].wait()
    spread = jnp.broadcast_to(p_inv, (ROWS, 128))
    inv_lane = jnp.concatenate([spread, spread], axis=0).T[0:8]
    lab_row = lab[...].astype(f32)
    lab_lane = jnp.broadcast_to(jnp.concatenate([lab_row, lab_row], axis=1), (8, 128))
    row8 = lax.broadcasted_iota(jnp.int32, (8, 128), 0)
    lane8 = lax.broadcasted_iota(jnp.int32, (8, 128), 1)
    meta = jnp.where(row8 == 0, inv_lane, jnp.where(row8 == 1, lab_lane, 0.0))
    M[me] = jnp.where(lane8 // ROWS == pa % 2, meta, 0.0)
    for ka in (2, 1, 3):
        send_m(ka)
    to_sib(0)
    for step in (0, 1):
        for d in (0, 1):
            send_u(0, 0, d ^ step, 0, (1, 3)[d])

    tacc[...] = jnp.zeros_like(tacc)
    svec[...] = jnp.zeros_like(svec)

    def fwd_b(ka, d):
        hf = d
        kb = (3, 1)[d]
        got_u(ka, kb, hf)
        send_u(ka, kb, hf, 0, (1, 3)[d])

    def along_b(ka, hf):
        got_u(ka, 0, hf)
        for d in ((0, 1) if hf == 0 else (1, 0)):
            send_u(ka, 0, hf, 0, (1, 3)[d])

    def meta_b():
        for ka in (1, 3, 2):
            got(("m", ka), M.at[slot(ka, 0)])
        for kb in (2, 1, 3):
            send(("ml", SIDE - kb), line(0), line(0), plane(0, kb))

    def row(kb):
        if kb:
            got(("ml", kb), line(kb))
        for ka in range(SIDE):
            if kb == 2:
                got_u(ka, 2, 0)
                got_u(ka, 2, 1)
            elif kb:
                got_u(ka, kb, 1 if kb == 3 else 0)

    m = mul[0]
    shift0 = shift[0]
    base = yh * 1024 + (group // 2) * 128
    k1 = m * LOG2E
    k2 = shift0 * LOG2E

    def lane_vec(v, r):
        return M[2 * v, r:r + 1] + M[2 * v + 1, r:r + 1]

    def transpose_texts(place, n):
        for side in (0, NZ):
            lo = (side + place) * ROWS
            flipped = T[side + place:side + place + n].reshape(n * ROWS, D).T
            Tt[:, :, lo:lo + n * ROWS] = flipped.reshape(8, FEAT, n * ROWS)

    def transpose_images(kb):
        b_ = (pb + kb) % SIDE
        flipped = U[pl.ds(b_ * SIDE, SIDE)].reshape(256, D).T
        for i in (0, 1):
            Ut[2 * b_ + i] = flipped[:, i * 128:(i + 1) * 128].reshape(8, FEAT, 128)

    def weights(place, n, kb):
        b_ = (pb + kb) % SIDE
        images = U[pl.ds(b_ * SIDE, SIDE)].reshape(256, D)
        label = jnp.concatenate([lane_vec(2 * b_, 1), lane_vec(2 * b_ + 1, 1)], axis=1)
        row = lax.broadcasted_iota(jnp.int32, (ROWS, 1), 0)
        size = n * ROWS
        for side in (0, 1):
            lo = (side * NZ + place) * ROWS
            rows = T[side * NZ + place:side * NZ + place + n].reshape(size, D)
            cos = lax.dot_general(rows, images, (((1,), (1,)), ((), ())), preferred_element_type=f32)
            owner = core if side == 0 else 1 - core
            ids = []
            for k in ORDER[place:place + n]:
                ids.append(row + ((z + k) % NZ * 2048 + base + owner * ROWS))
            match = jnp.concatenate(ids, axis=0).astype(f32) == label
            logit = cos * k1 + k2
            e = jnp.exp2(jnp.where(match, logit, -logit))
            w = (jnp.where(match, -m, m) / (1.0 + e)).astype(bf16)
            wc = w.astype(f32) * cos
            total = jnp.sum(wc, axis=0, keepdims=True)
            for i in (0, 1):
                cut = slice(i * 128, (i + 1) * 128)
                W[2 * b_ + i, lo:lo + size] = w[:, cut]
                svec[2 * b_ + i] += jnp.broadcast_to(total[:, cut], (8, 128))
            tacc[lo:lo + size] += wc[:, :128] + wc[:, 128:]

    got_t(7, 0)
    send_t(7, 0, 0)
    got_t(1, 1)
    send_t(1, 1, 1)
    got_t(7, 1)
    send_t(7, 1, 0)
    got_t(1, 0)
    send_t(1, 0, 1)
    to_sib(7)
    to_sib(1)
    along_b(3, 0)
    along_b(1, 1)
    along_b(2, 0)
    along_b(2, 1)
    fwd_b(0, 0)
    fwd_b(0, 1)
    along_b(3, 1)
    along_b(1, 0)
    meta_b()
    got_t(6, 0)
    send_t(6, 0, 0)
    got_t(2, 1)
    send_t(2, 1, 1)
    got_t(6, 1)
    send_t(6, 1, 0)
    got_t(2, 0)
    send_t(2, 0, 1)
    to_sib(6)
    to_sib(2)
    got_sib(1)
    got_sib(7)
    got_sib(0)
    row(0)
    weights(5, 3, 0)
    fwd_b(2, 0)
    fwd_b(2, 1)
    fwd_b(3, 0)
    fwd_b(1, 1)
    got_t(5, 0)
    send_t(5, 0, 0)
    got_t(3, 1)
    send_t(3, 1, 1)
    fwd_b(3, 1)
    fwd_b(1, 0)
    got_sib(2)
    got_sib(6)
    weights(3, 2, 0)
    got_t(5, 1)
    to_sib(5)
    got_t(3, 0)
    to_sib(3)
    transpose_texts(5, 3)
    transpose_texts(3, 2)
    transpose_images(0)
    row(1)
    row(3)
    weights(5, 3, 1)
    weights(5, 3, 3)
    weights(3, 2, 1)
    weights(3, 2, 3)
    transpose_images(1)
    transpose_images(3)
    got_t4()
    got_sib(3)
    got_sib(5)
    weights(0, 3, 0)
    weights(0, 3, 1)
    weights(0, 3, 3)
    transpose_texts(0, 3)
    row(2)
    weights(0, 8, 2)
    transpose_images(2)

    def text_part(place, n):
        rows = slice(place * ROWS, (place + n) * ROWS)
        lhs = jnp.concatenate([W[u, rows] for u in range(8)], axis=1)
        up = jnp.dot(lhs, U[...].reshape(1024, D), preferred_element_type=f32)
        along = jnp.sum(tacc[rows], axis=1, keepdims=True)
        unit = T[place:place + n].reshape(n * ROWS, D).astype(f32)
        return (up - unit * along).reshape(n, 2, HALF, D)

    def sib_part(place, n):
        cut = slice(place, place + n)
        sib_out[cut] = text_part(NZ + place, n).astype(bf16)
        send(("s", place), sib_out.at[cut], sib_in.at[cut], sib)

    def got_part(place, n):
        got(("s", place), sib_in.at[place:place + n])

    def own_part(place, n):
        own[place:place + n] = text_part(place, n)

    def image_part(kb, u):
        b_ = (pb + kb) % SIDE
        h = jnp.where(first, b_ // 2, u)
        units = [jnp.where(first, 4 * h + i, 2 * i + h) for i in range(4)]
        gs = [jnp.where(first, b_ % 2 * 4 + 2 * u + j, j * 4 + b_) for j in (0, 1)]
        lhs = jnp.concatenate([Tt[g] for g in gs], axis=0)
        rhs = jnp.concatenate([W[v] for v in units], axis=1)
        up = jnp.dot(lhs, rhs, preferred_element_type=f32)
        for hf in (0, 1):
            pair = units[2 * hf:2 * hf + 2]
            along = jnp.concatenate([svec[v][0:1] for v in pair], axis=1)
            inv = jnp.concatenate([lane_vec(v, 0) for v in pair], axis=1)
            for j, g in enumerate(gs):
                unit = jnp.concatenate([Ut[v, g] for v in pair], axis=1).astype(f32)
                part = up[j * FEAT:(j + 1) * FEAT, hf * 256:(hf + 1) * 256]
                G[kb, 2 * u + j, hf] = ((part - unit * along) * inv).astype(bf16)

    def a_at(ka):
        return (pa + ka) % SIDE

    def gb_far(ka):
        for d in (0, 1):
            send(("gh", ka, d), G.at[2, a_at(ka), d], rbh.at[ka, d], b_dev[d])

    def gb_fresh(d):
        kb = (1, 3)[d]
        send(("gn", d), G.at[kb, :, 1 - d], rbn.at[d], b_dev[d])

    def gb_near(d, ka):
        kb = (1, 3)[d]
        got(("gh", ka, d), rbh.at[ka, d])
        G[kb, a_at(ka), d] = (G[kb, a_at(ka), d].astype(f32) + rbh[ka, d].astype(f32)).astype(bf16)
        send(("gf", ka, d), G.at[kb, a_at(ka), d], rbf.at[ka, d], b_dev[d])

    def gb_sum(ka):
        halves = []
        for hf in (0, 1):
            if ka == 2:
                got(("gn", 1 - hf), rbn.at[1 - hf])
            got(("gf", ka, hf), rbf.at[ka, hf])
            halves.append(G[0, a_at(ka), hf].astype(f32) + rbf[ka, hf].astype(f32)
                          + rbn[1 - hf, a_at(ka)].astype(f32))
        return jnp.stack(halves)

    def text_sum(k, hf):
        p = PLACE[k]
        return own[p, hf] + sib_in[p, hf].astype(f32)

    def text_step(i, d, hf):
        k = (4 - i if d == 0 else 4 + i) % NZ
        value = text_sum(k, hf)
        if i > 1 or (i == 1 and hf == d):
            got(("r", d, i - 1, hf), trecv.at[d, i - 1, hf])
            value = value + trecv[d, i - 1, hf].astype(f32)
        tstage[d, i, hf] = value.astype(bf16)
        send(("r", d, i, hf), tstage.at[d, i, hf], trecv.at[d, i, hf], z_dev[d])

    def feature_halves(total, dst):
        for c in (0, 1):
            rows = jnp.concatenate([total[:, c * PART:(c + 1) * PART], jnp.zeros((2, PAD - PART, 256), f32)], axis=1)
            dst[c] = rows.astype(bf16)

    def along_a(ka):
        feature_halves(gb_sum(ka), r1.at[ka])
        i = at(("ga", 0, ka))
        at(("ga", 1, ka))
        for c in (0, 1):
            j = at(("ga to", c, ka))
            copy = rdma(r1.at[ka, c], ra.at[core, ka - 1], ssem.at[j], rsem.at[i + core], plane(ka, 0, c))
            copy.start()
            started.append(copy)

    def own_a():
        total = gb_sum(0)
        feature_halves(total, r1.at[0])
        for c in (0, 1):
            fin[c] = total[:, c * PART:(c + 1) * PART]
        send(("gs",), r1.at[0, 1 - core], ra_sib, sib)

    def image_end():
        got(("gs",), ra_sib)
        mine = fin[core]
        other = ra_sib[:, :PART].astype(f32)
        sums = [jnp.where(first, mine, other), jnp.where(first, other, mine)]
        for ka in (2, 1, 3):
            for c in (0, 1):
                got(("ga", c, ka), ra.at[c, ka - 1])
                sums[c] = sums[c] + ra[c, ka - 1, :, :PART].astype(f32)
        even, odd = sums
        blocks = []
        for g in range(8):
            for half, j in ((even, g), (odd, g % 4 * 2 + g // 4)):
                lo = (j % 4) * ROWS
                blocks.append(half[j // 4][:, lo:lo + ROWS])
        img_out[...] = jnp.concatenate(blocks, axis=1).astype(bf16)

    def text_end(hf):
        value = text_sum(0, hf)
        for d in (0, 1):
            got(("r", d, 3, hf), trecv.at[d, 3, hf])
            value = value + trecv[d, 3, hf].astype(f32)
        txt_out[hf * HALF:(hf + 1) * HALF] = value * t_inv[hf * HALF:(hf + 1) * HALF]

    u_far = (pa + 2) % SIDE // 2
    order = (2, 1, 3, 0)

    def image_parts(kb):
        @pl.loop(0, 2)
        def _(u):
            image_part(kb, u)

    image_part(2, u_far)
    gb_far(2)
    image_part(2, 1 - u_far)
    for ka in (1, 3, 0):
        gb_far(ka)
    sib_part(0, 3)
    own_part(0, 3)
    got_part(0, 3)
    text_step(0, 0, 0)
    text_step(0, 1, 1)
    text_step(1, 0, 1)
    text_step(1, 1, 0)
    image_parts(1)
    gb_fresh(0)
    image_parts(3)
    gb_fresh(1)
    for ka in order:
        for d in (0, 1):
            gb_near(d, ka)
    text_step(1, 0, 0)
    text_step(1, 1, 1)
    sib_part(3, 5)
    own_part(3, 5)
    got_part(3, 5)
    text_step(2, 0, 1)
    text_step(2, 1, 0)
    image_parts(0)
    text_step(2, 0, 0)
    text_step(2, 1, 1)
    for ka in (2, 1, 3):
        along_a(ka)
    text_step(3, 0, 1)
    text_step(3, 1, 0)
    own_a()
    text_step(3, 0, 0)
    text_step(3, 1, 1)
    image_end()
    text_end(0)
    text_end(1)

    for copy in started:
        copy.wait_send()


def local(picture_embeds, caption_embeds, positive_caption_ids, logit_multiplier, logit_shift):
    vmem = pl.BlockSpec(memory_space=pltpu.VMEM)
    hbm = pl.BlockSpec(memory_space=pltpu.HBM)
    smem = pl.BlockSpec(memory_space=pltpu.SMEM)
    dma = pltpu.SemaphoreType.DMA
    scratch = [
        pltpu.VMEM((ROWS, D), bf16),
        pltpu.VMEM((ROWS, D), bf16),
        pltpu.VMEM((1, ROWS), jnp.int32),
        pltpu.VMEM((16, 2, HALF, D), bf16),
        pltpu.VMEM((16, 8, 128), f32),
        pltpu.VMEM((16, 2, HALF, D), bf16),
        pltpu.VMEM((8, 8, FEAT, 128), bf16),
        pltpu.VMEM((8, FEAT, 1024), bf16),
        pltpu.VMEM((8, 1024, 128), bf16),
        pltpu.VMEM((1024, 128), f32),
        pltpu.VMEM((8, 8, 128), f32),
        pltpu.VMEM((NZ, 2, HALF, D), f32),
        pltpu.VMEM((NZ, 2, HALF, D), bf16),
        pltpu.VMEM((NZ, 2, HALF, D), bf16),
        pltpu.VMEM((2, 4, 2, HALF, D), bf16),
        pltpu.VMEM((2, 4, 2, HALF, D), bf16),
        pltpu.VMEM((4, 4, 2, FEAT, 256), bf16),
        pltpu.VMEM((4, 2, FEAT, 256), bf16),
        pltpu.VMEM((4, 2, FEAT, 256), bf16),
        pltpu.VMEM((2, 4, FEAT, 256), bf16),
        pltpu.VMEM((2, 3, 2, PAD, 256), bf16),
        pltpu.VMEM((2, PAD, 256), bf16),
        pltpu.VMEM((4, 2, 2, PAD, 256), bf16),
        pltpu.VMEM((2, 2, PART, 256), f32),
        dma((N_SEM,)), dma((N_SEM,)), dma((3,)),
    ]
    return pl.pallas_call(
        kernel,
        out_shape=(jax.ShapeDtypeStruct((PART, 1024), bf16), jax.ShapeDtypeStruct((ROWS, D), f32)),
        in_specs=[hbm, hbm, hbm, smem, smem],
        out_specs=(vmem, vmem),
        scratch_shapes=scratch,
        compiler_params=pltpu.CompilerParams(
            collective_id=0, has_side_effects=True, vmem_limit_bytes=VMEM_MIB * 2**20),
        cost_estimate=pl.CostEstimate(flops=7 * 10**9, bytes_accessed=10**6, transcendentals=2**20),
    )(*(pltpu.with_memory_space_constraint(v, pltpu.HBM) for v in (
        picture_embeds, caption_embeds, positive_caption_ids.reshape(1, ROWS))), logit_multiplier, logit_shift)


def solution(mesh):
    placed = (P(("batch", "group"), None), P(("batch", "group"), None), P(("batch", "group")), P(), P())
    return jax.shard_map(
        local, mesh=mesh, in_specs=placed,
        out_specs=(P("group", "batch"), P(("batch", "group"), None)), check_vma=False)
```
